32 devices in a mesh: group: 4 (over z), dev: 8 (over y, x, core).
Axes of the slice: x: 2, y: 2, z: 4, core: 2. Of those that a mesh axis runs over, the one named last changes fastest.
Arguments:
- points: bfloat16 [49152, 512], P(('group', 'dev')), may hold values from -5 to 5
- targets: float32 [8, 49152], P(None, ('group', 'dev')), may hold values from -16 to 16
- partner_tiles: int32 [4, 8, 4, 2], replicated, may hold values from -1 to 5, as said below
Outputs:
- solution: float32 [8, 49152], P(None, ('group', 'dev'))
- residual: float32 [8, 49152], P(None, ('group', 'dev'))
The draws below stay inside these ranges and needn't reach their ends.
Inputs may be any that keep to these rules, and one draw needn't show every extreme that they name: `partner_tiles`: entry [g, v, h, c] names a tile of block (h, v) whose points are coupled with every point of block (g, v), or is -1. For one v and two groups at most one of the two blocks names tiles of the other, and no block names tiles of its own group. The tiles named in [g, v, h] are distinct and stand before its -1 entries. In every draw some block names 2 tiles of one other group.
All inputs are finite; a program needn't handle non-finite values.
Results may differ from the reference program's by a relative error of at most 0.0003.
Values may be sent and summed in bfloat16 or wider, within the bound.
A program may use at most 192 MiB of HBM per device.

```python
import jax
import jax.numpy as jnp
from jax import lax

D = 512
TILE = 256
TILES_DEV = 6
PROBES = 8
CAP = 2
ITERS = 2
POINTS = 49152
N_GROUP = 4
N_DEV = 8


def draw_points(key, part):
    latent_key, jitter_key, flip_key = jax.random.split(key, 3)
    latent_scale = (4.0 / D) ** 0.5
    jitter_scale = (1.28 / D) ** 0.5
    latent = jnp.clip(jax.random.normal(latent_key, (POINTS, 8), jnp.float32), -4.0, 4.0) * latent_scale
    jitter = jnp.clip(jax.random.normal(jitter_key, (POINTS, D), jnp.float32), -4.0, 4.0) * jitter_scale
    flips = (jax.random.randint(flip_key, (D,), 0, 2) * 2 - 1).astype(jnp.float32)
    columns = jnp.arange(D) % 8
    return (latent[:, columns] * flips[None, :] + jitter).astype(jnp.bfloat16)


def draw_targets(key, part):
    fraction = jnp.arange(POINTS).astype(jnp.float32)[None, :] / POINTS
    values = jnp.clip(jax.random.normal(key, (PROBES, POINTS), jnp.float32), -5.0, 5.0) * (1.0 + 2.0 * fraction)
    return values


def draw_partner_tiles(key, part):
    weight_key = jax.random.fold_in(key, 0)
    start_key = jax.random.fold_in(key, 3)
    weights = jax.random.randint(weight_key, (N_GROUP, N_DEV), 0, 1 << 20)
    start_tile = jax.random.randint(start_key, (N_GROUP, N_GROUP, N_DEV), 0, TILES_DEV)
    own_group = jnp.arange(N_GROUP)[:, None, None] + jnp.zeros((N_GROUP, N_GROUP, N_DEV), jnp.int32)
    peer_group = jnp.arange(N_GROUP)[None, :, None] + jnp.zeros((N_GROUP, N_GROUP, N_DEV), jnp.int32)
    dev_index = jnp.arange(N_DEV)[None, None, :] + jnp.zeros((N_GROUP, N_GROUP, N_DEV), jnp.int32)
    lower_group = jnp.minimum(own_group, peer_group)
    upper_group = jnp.maximum(own_group, peer_group)
    own_weight = weights[own_group, dev_index]
    peer_weight = weights[peer_group, dev_index]
    owns_pair = jnp.logical_or(own_weight > peer_weight, jnp.logical_and(own_weight == peer_weight, own_group < peer_group))
    listed = jnp.logical_and(owns_pair, own_group != peer_group)
    slot_range = jnp.arange(CAP)[None, None, None, :]
    filled = jnp.logical_and(listed[..., None], slot_range < CAP)
    tiles_named = jnp.where(filled, (start_tile[lower_group, upper_group, dev_index][..., None] + slot_range) % TILES_DEV, -1)
    return jnp.transpose(tiles_named, (0, 2, 1, 3)).astype(jnp.int32)


def setup_inputs(seed: int = 0) -> dict:
    splits = jax.random.split(jax.random.key(seed), 4)
    return {
        "points": draw_points(jax.random.fold_in(splits[3], 71), 0),
        "targets": draw_targets(jax.random.fold_in(splits[3], 71), 0),
        "partner_tiles": draw_partner_tiles(jax.random.fold_in(splits[3], 71), 0),
    }


length_scale = 3.9
noise_level = 1.0
coupling_weight = 0.5
highest = lax.Precision.HIGHEST

def affinity(left_points, right_points, left_norms, right_norms):
    inner_prod = lax.dot_general(left_points, right_points, (((1,), (1,)), ((), ())), preferred_element_type=jnp.float32)
    dist_sq = jnp.maximum(left_norms[:, None] + right_norms[None, :] - 2.0 * inner_prod, 0.0)
    scaled = jnp.sqrt(dist_sq) / length_scale
    return jnp.maximum(1.0 - scaled, 0.0) ** 4 * (4.0 * scaled + 1.0)

def contract_last(left_values, right_values):
    return lax.dot_general(left_values, right_values, (((1,), (1,)), ((), ())), precision=highest, preferred_element_type=jnp.float32)

def add_rows(accumulated, start, addition):
    axis_last = accumulated.ndim - 1
    current = lax.dynamic_slice_in_dim(accumulated, start, addition.shape[-1], axis_last)
    return lax.dynamic_update_slice_in_dim(accumulated, current + addition, start, axis_last)

def couple_all(points, row_norms, vector, partner_tiles):
    row_count = TILES_DEV * TILE

    def visit(running, device):
        degree, coupled = running
        group_index = device // N_DEV
        position = device % N_DEV
        start = (device * row_count).astype(jnp.int32)
        own_points = lax.dynamic_slice_in_dim(points, start, row_count, 0)
        own_sq = lax.dynamic_slice_in_dim(row_norms, start, row_count, 0)
        own_vector = lax.dynamic_slice_in_dim(vector, start, row_count, 1)
        local_block = affinity(own_points, own_points, own_sq, own_sq)
        own_degree = lax.optimization_barrier(jnp.sum(local_block, axis=1))
        own_coupled = contract_last(own_vector, local_block)

        def pair_with(totals, remote_start, size):
            degree_now, coupled_now, degree_own, coupled_own = totals
            remote_points = lax.dynamic_slice_in_dim(points, remote_start, size, 0)
            remote_sq = lax.dynamic_slice_in_dim(row_norms, remote_start, size, 0)
            remote_vector = lax.dynamic_slice_in_dim(vector, remote_start, size, 1)
            blocks = affinity(own_points, remote_points, own_sq, remote_sq)
            degree_own = degree_own + lax.optimization_barrier(jnp.sum(blocks, axis=1))
            coupled_own = coupled_own + contract_last(remote_vector, blocks)
            degree_now = add_rows(degree_now, remote_start, lax.optimization_barrier(jnp.sum(blocks, axis=0)))
            coupled_now = add_rows(coupled_now, remote_start, jnp.dot(own_vector, blocks, precision=highest, preferred_element_type=jnp.float32))
            return (degree_now, coupled_now, degree_own, coupled_own)
        totals = (degree, coupled, own_degree, own_coupled)
        for offset in (1, 2):
            remote_start = (jnp.maximum(device - offset, 0) * row_count).astype(jnp.int32)
            totals = lax.cond(position >= offset, lambda held: pair_with(held, remote_start, row_count), lambda held: held, totals)
        own_list = lax.dynamic_index_in_dim(lax.dynamic_index_in_dim(partner_tiles, group_index, 0, keepdims=False), position, 0, keepdims=False)
        for partner in range(N_GROUP):
            for column in range(CAP):
                tile_id = own_list[partner, column]
                remote_start = ((partner * N_DEV + position) * row_count + jnp.maximum(tile_id, 0) * TILE).astype(jnp.int32)
                totals = lax.cond(tile_id >= 0, lambda held: pair_with(held, remote_start, TILE), lambda held: held, totals)
        degree, coupled, own_degree, own_coupled = totals
        degree = add_rows(degree, start, own_degree)
        coupled = add_rows(coupled, start, own_coupled)
        return ((degree, coupled), None)
    initial = (jnp.zeros((POINTS,), jnp.float32), jnp.zeros((PROBES, POINTS), jnp.float32))
    (degree, coupled), unused = lax.scan(visit, initial, jnp.arange(N_GROUP * N_DEV, dtype=jnp.int32))
    return (degree, coupled)

def reference(points, targets, partner_tiles):
    row_norms = lax.optimization_barrier(jnp.sum(jnp.square(points.astype(jnp.float32)), axis=1))
    degree, coupled = couple_all(points, row_norms, targets, partner_tiles)

    def operate(vector, coupled_part):
        return noise_level * vector + coupling_weight * (degree[None, :] * vector - coupled_part)
    solution = jnp.zeros_like(targets)
    residual = targets
    direction = targets
    applied = operate(targets, coupled)
    norm_now = lax.optimization_barrier(jnp.sum(residual * residual, axis=1))
    for iteration in range(ITERS):
        if iteration > 0:
            unused, coupled = couple_all(points, row_norms, direction, partner_tiles)
            applied = operate(direction, coupled)
        curvature = lax.optimization_barrier(jnp.sum(direction * applied, axis=1))
        step_size = norm_now / curvature
        solution = solution + step_size[:, None] * direction
        residual = residual - step_size[:, None] * applied
        if iteration + 1 < ITERS:
            norm_next = lax.optimization_barrier(jnp.sum(residual * residual, axis=1))
            direction = residual + (norm_next / norm_now)[:, None] * direction
            norm_now = norm_next
    return (solution, residual)
```

```python
import functools

import jax
import jax.numpy as jnp
from jax import lax
from jax.experimental import pallas as pl
from jax.experimental.pallas import tpu as pltpu
from jax.sharding import PartitionSpec as P

TILE = 256

length_scale = 3.9
noise_level = 1.0
coupling_weight = 0.5
MESH = pl.DeviceIdType.MESH
NT = (((1,), (1,)), ((), ()))
NN = (((1,), (0,)), ((), ()))


def mxu(left, right, dims):
    return lax.dot_general(left, right, dims, preferred_element_type=jnp.float32)


def split_rows(values, ones):
    high = values.astype(jnp.bfloat16).astype(jnp.float32)
    pieces = [high, values - high]
    if ones:
        pieces += [jnp.ones_like(values), jnp.zeros_like(values)]
    return jnp.concatenate(pieces, axis=0).astype(jnp.bfloat16)


def merge_rows(summed, probes, ones):
    coupled = summed[0:probes] + summed[probes : 2 * probes]
    if ones:
        return jnp.concatenate([coupled, summed[2 * probes : 3 * probes]], axis=0)
    return coupled


def kernel(groups, devs, cap, probes, tiles,
           tab, pts, tgt, sol, res,
           pin, outp, inp, kmat, kc, ncol, vec1, vin1, cvo1, cvi1, vec2, vin2, cvo2, cvi2,
           hout1, hin1, cho1, chi1, hout2, hin2, cho2, chi2,
           mown, mtile, mrem, mc, acc, red1o, red1, red2o, red2,
           psend, precv, cpsend, cprecv, vsend, vrecv, cvsend, cvrecv,
           hsend, hrecv, chsend, chrecv, r1send, r1recv, r2send, r2recv):
    g = lax.axis_index("group")
    d = lax.axis_index("dev")
    par = lax.rem(d, 2)
    odd = par == 1
    even = par == 0
    peers = groups - 1
    cols = tiles * TILE

    def tile_id(owner, other, c):
        return tab[((owner * devs + d) * groups + other) * cap + c]

    def up(k):
        return lax.rem(g + k, groups)

    def down(k):
        return lax.rem(g + groups - k, groups)

    def cs(j):
        return slice(j * TILE, (j + 1) * TILE)

    @pl.loop(0, tiles)
    def _(i):
        wide = pts[i].astype(jnp.float32)
        ncol[i] = jnp.sum(wide * wide, axis=1, keepdims=True)

    for j in range(tiles):
        wide = pts[j].astype(jnp.float32)
        squares = wide * wide
        high = squares.astype(jnp.bfloat16)
        low = (squares - high.astype(jnp.float32)).astype(jnp.bfloat16)
        ones = jnp.ones((16, wide.shape[1]), jnp.bfloat16)
        sums = mxu(ones, high, NT) + mxu(ones, low, NT)
        vec1[0:probes, cs(j)] = tgt[:, cs(j)]
        vec1[probes : 2 * probes, cs(j)] = sums[0:probes]
        rows = split_rows(tgt[:, cs(j)], True)
        mown[:, cs(j)] = rows
        mtile[j] = rows
    for k in range(1, groups):
        for c in range(cap):
            named = tile_id(up(k), g, c)
            outp[k - 1, c] = pts[jnp.maximum(named, 0)]
            total = jnp.zeros((2 * probes, TILE), jnp.float32)
            for q in range(tiles):
                total = total + jnp.where(named == q, 1.0, 0.0) * vec1[:, cs(q)]
            cvo1[k - 1, :, cs(c)] = total

    barrier = pltpu.get_barrier_semaphore()
    for k in range(1, groups):
        pl.semaphore_signal(barrier, inc=1, device_id={"group": up(k)}, device_id_type=MESH)
    for k in range(1, devs):
        pl.semaphore_signal(barrier, inc=1, device_id={"dev": lax.rem(d + k, devs)}, device_id_type=MESH)
    pl.semaphore_wait(barrier, groups + devs - 2)

    def remote(src, dst, ssem, rsem, where):
        return pltpu.make_async_remote_copy(
            src_ref=src, dst_ref=dst, send_sem=ssem, recv_sem=rsem, device_id=where, device_id_type=MESH
        )

    has_next = d + 1 < devs
    far = jnp.where(odd, jnp.minimum(d + 2, devs - 1), jnp.maximum(d - 2, 0))
    has_far = jnp.logical_or(jnp.logical_and(odd, d + 2 < devs), jnp.logical_and(even, d >= 2))
    nxt = jnp.minimum(d + 1, devs - 1)
    has_first = jnp.logical_or(odd, d + 2 < devs)
    has_second = d >= 2
    first_owner = jnp.where(odd, jnp.maximum(d - 1, 0), jnp.minimum(d + 2, devs - 1))
    second_owner = jnp.where(odd, jnp.maximum(d - 2, 0), jnp.maximum(d - 1, 0))
    has_block = (has_first, has_second)
    block_owner = (first_owner, second_owner)
    block_slot = (1 - par, par)

    def vec_copy(r, which):
        src, dst = (vec1, vin1) if r == 0 else (vec2, vin2)
        return remote(src, dst.at[par], vsend.at[r, which], vrecv.at[r, par], {"dev": (nxt, far)[which]})

    def vec_in(r, block):
        src, dst = (vec1, vin1) if r == 0 else (vec2, vin2)
        return remote(src, dst.at[block], vsend.at[r, 0], vrecv.at[r, block], {"dev": nxt})

    def cvec(r, k):
        src, dst = (cvo1, cvi1) if r == 0 else (cvo2, cvi2)
        return remote(src.at[k - 1], dst.at[k - 1], cvsend.at[r, k - 1], cvrecv.at[r, k - 1], {"group": up(k)})

    def hand(r, block):
        src, dst = (hout1, hin1) if r == 0 else (hout2, hin2)
        slot = block_slot[block]
        return remote(src.at[block], dst.at[slot], hsend.at[r, block], hrecv.at[r, slot],
                      {"dev": block_owner[block]})

    def hand_in(r, slot):
        src, dst = (hout1, hin1) if r == 0 else (hout2, hin2)
        return remote(src.at[0], dst.at[slot], hsend.at[r, 0], hrecv.at[r, slot], {"dev": nxt})

    def chand(r, k):
        src, dst = (cho1, chi1) if r == 0 else (cho2, chi2)
        return remote(src.at[k - 1], dst.at[k - 1], chsend.at[r, k - 1], chrecv.at[r, k - 1], {"group": down(k)})

    def cpts(k):
        return remote(outp.at[k - 1], inp.at[k - 1], cpsend.at[k - 1], cprecv.at[k - 1], {"group": up(k)})

    far_pts = remote(pts, pin.at[par], psend.at[1], precv.at[par], {"dev": far})
    mate_pts = remote(pts, pin.at[0], psend.at[0], precv.at[0], {"dev": nxt})
    forward_pts = remote(pin.at[1], pin.at[1], psend.at[0], precv.at[1], {"dev": jnp.maximum(d - 1, 0)})

    def send_vectors(r):
        for which, cond in ((0, has_next), (1, has_far)):
            @pl.when(cond)
            def _():
                vec_copy(r, which).start()
        for k in range(1, groups):
            cvec(r, k).start()

    send_vectors(0)
    for k in range(1, groups):
        cpts(k).start()

    @pl.when(has_far)
    def _():
        far_pts.start()

    @pl.when(even)
    def _():
        mate_pts.start()

    def affinity(own, norm_col, other, norm_row):
        inner = mxu(own, other, NT)
        dist_sq = jnp.maximum(norm_col + norm_row - 2.0 * inner, 0.0)
        scaled = dist_sq * lax.rsqrt(jnp.maximum(dist_sq, 1e-30)) * (1.0 / length_scale)
        near = jnp.maximum(1.0 - scaled, 0.0)
        near = near * near
        return near * near * (4.0 * scaled + 1.0)

    @pl.loop(0, tiles)
    def _(i):
        total = jnp.zeros((4 * probes, TILE), jnp.float32)
        for j in range(tiles):
            value = affinity(pts[i], ncol[i], pts[j], vec1[probes : probes + 1, cs(j)]).astype(jnp.bfloat16)
            kmat[0, i, :, cs(j)] = value
            total = total + mxu(mown[:, cs(j)], value, NT)
        acc[i] = total

    def band(block):
        vec_in(0, block).wait_recv()
        for j in range(tiles):
            mrem[:, cs(j)] = split_rows(vin1[block, 0:probes, cs(j)], True)
        hout1[block] = jnp.zeros((2 * probes, cols), jnp.float32)

        @pl.loop(0, tiles)
        def _(i):
            total = acc[i]
            for j in range(tiles):
                value = affinity(
                    pts[i], ncol[i], pin[block, j], vin1[block, probes : probes + 1, cs(j)]
                ).astype(jnp.bfloat16)
                kmat[1 + block, i, :, cs(j)] = value
                total = total + mxu(mrem[:, cs(j)], value, NT)
                hout1[block, :, cs(j)] += merge_rows(mxu(mtile[i], value, NN), probes, True)
            acc[i] = total

        hand(0, block).start()

    def cross(k):
        cvec(0, k).wait_recv()
        cpts(k).wait_recv()
        live = [jnp.where(tile_id(g, down(k), c) >= 0, 1.0, 0.0) for c in range(cap)]
        for c in range(cap):
            mc[k - 1, :, cs(c)] = split_rows(cvi1[k - 1, 0:probes, cs(c)], True)
        cho1[k - 1] = jnp.zeros((2 * probes, cap * TILE), jnp.float32)

        @pl.loop(0, tiles)
        def _(i):
            total = acc[i]
            for c in range(cap):
                value = affinity(
                    pts[i], ncol[i], inp[k - 1, c], cvi1[k - 1, probes : probes + 1, cs(c)]
                )
                value = (value * live[c]).astype(jnp.bfloat16)
                kc[k - 1, i, :, cs(c)] = value
                total = total + mxu(mc[k - 1, :, cs(c)], value, NT)
                cho1[k - 1, :, cs(c)] += merge_rows(mxu(mtile[i], value, NN), probes, True)
            acc[i] = total

        chand(0, k).start()

    @pl.when(has_first)
    def _():
        remote(pts, pin.at[0], psend.at[0], precv.at[0], {"dev": nxt}).wait_recv()
        band(0)

    cross(1)

    @pl.when(has_second)
    def _():
        remote(pts, pin.at[1], psend.at[0], precv.at[1], {"dev": nxt}).wait_recv()

        @pl.when(odd)
        def _():
            forward_pts.start()

        band(1)

    for k in range(2, groups):
        cross(k)

    def gather_backs(r, total):
        incoming, cross_in = (hin1, chi1) if r == 0 else (hin2, chi2)
        for k in range(1, groups):
            chand(r, k).wait_recv()
        for k in range(1, groups):
            for c in range(cap):
                named = tile_id(up(k), g, c)
                part = cross_in[k - 1, :, cs(c)]
                for q in range(tiles):
                    total[q] = total[q] + jnp.where(named == q, 1.0, 0.0) * part
        return total

    def wait_hands(r):
        for slot, cond in ((0, has_next), (1, has_far)):
            @pl.when(cond)
            def _():
                hand_in(r, slot).wait_recv()

    incoming_ok = [jnp.where(has_next, 1.0, 0.0), jnp.where(has_far, 1.0, 0.0)]
    for slot, cond in ((0, has_next), (1, has_far)):
        @pl.when(jnp.logical_not(cond))
        def _():
            hin1[slot] = jnp.zeros((2 * probes, cols), jnp.float32)
            hin2[slot] = jnp.zeros((probes, cols), jnp.float32)

    wait_hands(0)
    sums = [merge_rows(acc[q], probes, True) + hin1[0, :, cs(q)] + hin1[1, :, cs(q)] for q in range(tiles)]
    sums = gather_backs(0, sums)
    for q in range(tiles):
        base = tgt[:, cs(q)]
        degree = sums[q][probes : 2 * probes]
        applied = noise_level * base + coupling_weight * (degree * base - sums[q][0:probes])
        vec2[:, cs(q)] = applied
        sol[:, cs(q)] = degree
    for k in range(1, groups):
        for c in range(cap):
            named = tile_id(up(k), g, c)
            total = jnp.zeros((probes, TILE), jnp.float32)
            for q in range(tiles):
                total = total + jnp.where(named == q, 1.0, 0.0) * vec2[:, cs(q)]
            cvo2[k - 1, :, cs(c)] = total
    send_vectors(1)

    for j in range(tiles):
        rows = split_rows(vec2[:, cs(j)], False)
        mown[0 : 2 * probes, cs(j)] = rows
        mtile[j, 0 : 2 * probes] = rows
    two = 2 * probes

    @pl.loop(0, tiles)
    def _(i):
        acc[i, 0:two] = mxu(mown[0:two], kmat[0, i], NT)

    def merged(q):
        return merge_rows(acc[q, 0:two], probes, False)

    quad_local = jnp.zeros((probes, 1), jnp.float32)
    for q in range(tiles):
        quad_local = quad_local + jnp.sum(vec2[:, cs(q)] * merged(q), axis=1, keepdims=True)

    def band_again(block):
        vec_in(1, block).wait_recv()
        for j in range(tiles):
            mrem[0:two, cs(j)] = split_rows(vin2[block, :, cs(j)], False)
        hout2[block] = jnp.zeros((probes, cols), jnp.float32)

        @pl.loop(0, tiles)
        def _(i):
            value = kmat[1 + block, i]
            acc[i, 0:two] += mxu(mrem[0:two], value, NT)
            hout2[block] += merge_rows(mxu(mtile[i, 0:two], value, NN), probes, False)

        hand(1, block).start()

    def cross_again(k):
        cvec(1, k).wait_recv()
        for c in range(cap):
            mc[k - 1, 0:two, cs(c)] = split_rows(cvi2[k - 1, :, cs(c)], False)
        cho2[k - 1] = jnp.zeros((probes, cap * TILE), jnp.float32)

        @pl.loop(0, tiles)
        def _(i):
            value = kc[k - 1, i]
            acc[i, 0:two] += mxu(mc[k - 1, 0:two], value, NT)
            cho2[k - 1] += merge_rows(mxu(mtile[i, 0:two], value, NN), probes, False)

        chand(1, k).start()

    for block in range(2):
        @pl.when(has_block[block])
        def _():
            band_again(block)

    for k in range(1, groups):
        cross_again(k)

    parts = [jnp.zeros((probes, 1), jnp.float32) for _ in range(5)]
    for q in range(tiles):
        base, applied, degree = tgt[:, cs(q)], vec2[:, cs(q)], sol[:, cs(q)]
        terms = (base * base, base * applied, applied * applied, degree * applied * applied, applied * merged(q))
        parts = [old + jnp.sum(term, axis=1, keepdims=True) for old, term in zip(parts, terms)]
    quad = 2.0 * parts[4] - quad_local
    curved = noise_level * parts[2] + coupling_weight * (parts[3] - quad)
    lane = lax.broadcasted_iota(jnp.int32, (probes, 128), 1)
    message = jnp.zeros((probes, 128), jnp.float32)
    for index, part in enumerate((parts[0], parts[1], parts[2], curved)):
        message = message + jnp.where(lane == index, part, 0.0)
    red1o[...] = message

    def reduce_one(k):
        return remote(red1o, red1.at[k - 1], r1send.at[k - 1], r1recv.at[k - 1], {"group": up(k)})

    def reduce_two(k):
        return remote(red2o, red2.at[k - 1], r2send.at[k - 1], r2recv.at[k - 1], {"dev": lax.rem(d + k, devs)})

    for k in range(1, groups):
        reduce_one(k).start()
    for k in range(1, groups):
        reduce_one(k).wait_recv()
    for k in range(1, groups):
        message = message + red1[k - 1]
    red2o[...] = message
    for k in range(1, devs):
        reduce_two(k).start()

    wait_hands(1)
    sums = [merged(q) + hin2[0, :, cs(q)] + hin2[1, :, cs(q)] for q in range(tiles)]
    sums = gather_backs(1, sums)
    for q in range(tiles):
        applied, degree = vec2[:, cs(q)], sol[:, cs(q)]
        res[:, cs(q)] = noise_level * applied + coupling_weight * (degree * applied - sums[q])
    for k in range(1, devs):
        reduce_two(k).wait_recv()
    for k in range(1, devs):
        message = message + red2[k - 1]
    norm0, curv0, app_sq, app_curv = [
        jnp.sum(jnp.where(lane == index, message, 0.0), axis=1, keepdims=True) for index in range(4)
    ]
    step0 = norm0 / curv0
    norm1 = norm0 - 2.0 * step0 * curv0 + step0 * step0 * app_sq
    mix = 1.0 + norm1 / norm0
    curv1 = mix * mix * curv0 - 2.0 * mix * step0 * app_sq + step0 * step0 * app_curv
    step1 = norm1 / curv1
    for q in range(tiles):
        base, applied, twice = tgt[:, cs(q)], vec2[:, cs(q)], res[:, cs(q)]
        sol[:, cs(q)] = step0 * base + step1 * (mix * base - step0 * applied)
        res[:, cs(q)] = (base - step0 * applied) - step1 * (mix * applied - step0 * twice)

    for r in range(2):
        for which, cond in ((0, has_next), (1, has_far)):
            @pl.when(cond)
            def _():
                vec_copy(r, which).wait_send()
        for block in range(2):
            @pl.when(has_block[block])
            def _():
                hand(r, block).wait_send()
        for k in range(1, groups):
            cvec(r, k).wait_send()
            chand(r, k).wait_send()
    for k in range(1, groups):
        cpts(k).wait_send()
        reduce_one(k).wait_send()
    for k in range(1, devs):
        reduce_two(k).wait_send()

    @pl.when(has_far)
    def _():
        far_pts.wait_send()

    @pl.when(even)
    def _():
        mate_pts.wait_send()

    @pl.when(jnp.logical_and(odd, has_second))
    def _():
        forward_pts.wait_send()


def on_device(points, targets, partner_tiles):
    groups, devs, _, cap = partner_tiles.shape
    rows, features = points.shape
    tiles = rows // TILE
    probes = targets.shape[0]
    peers = groups - 1
    f32, bf16 = jnp.float32, jnp.bfloat16
    v = pltpu.VMEM
    dma = pltpu.SemaphoreType.DMA
    wide = cap * TILE
    two = 2 * probes
    scratch = [
        v((2, tiles, TILE, features), bf16),
        v((peers, cap, TILE, features), bf16),
        v((peers, cap, TILE, features), bf16),
        v((3, tiles, TILE, rows), bf16),
        v((peers, tiles, TILE, wide), bf16),
        v((tiles, TILE, 1), f32),
        v((two, rows), f32),
        v((2, two, rows), f32),
        v((peers, two, wide), f32),
        v((peers, two, wide), f32),
        v((probes, rows), f32),
        v((2, probes, rows), f32),
        v((peers, probes, wide), f32),
        v((peers, probes, wide), f32),
        v((2, two, rows), f32),
        v((2, two, rows), f32),
        v((peers, two, wide), f32),
        v((peers, two, wide), f32),
        v((2, probes, rows), f32),
        v((2, probes, rows), f32),
        v((peers, probes, wide), f32),
        v((peers, probes, wide), f32),
        v((2 * two, rows), bf16),
        v((tiles, 2 * two, TILE), bf16),
        v((2 * two, rows), bf16),
        v((peers, 2 * two, wide), bf16),
        v((tiles, 2 * two, TILE), f32),
        v((probes, 128), f32),
        v((peers, probes, 128), f32),
        v((probes, 128), f32),
        v((devs - 1, probes, 128), f32),
        dma((2,)), dma((2,)), dma((peers,)), dma((peers,)),
        dma((2, 2)), dma((2, 2)), dma((2, peers)), dma((2, peers)),
        dma((2, 2)), dma((2, 2)), dma((2, peers)), dma((2, peers)),
        dma((peers,)), dma((peers,)), dma((devs - 1,)), dma((devs - 1,)),
    ]
    pairs = rows * rows * 3 + rows * wide * peers
    return pl.pallas_call(
        functools.partial(kernel, groups, devs, cap, probes, tiles),
        out_shape=(jax.ShapeDtypeStruct(targets.shape, f32), jax.ShapeDtypeStruct(targets.shape, f32)),
        in_specs=[
            pl.BlockSpec(memory_space=pltpu.SMEM),
            pl.BlockSpec(memory_space=pltpu.VMEM),
            pl.BlockSpec(memory_space=pltpu.VMEM),
        ],
        out_specs=(pl.BlockSpec(memory_space=pltpu.VMEM), pl.BlockSpec(memory_space=pltpu.VMEM)),
        scratch_shapes=scratch,
        compiler_params=pltpu.CompilerParams(
            collective_id=0, has_side_effects=True, vmem_limit_bytes=56 * 1024 * 1024
        ),
        cost_estimate=pl.CostEstimate(flops=2 * features * pairs, bytes_accessed=rows * features * 2, transcendentals=pairs),
        name="graph_cg",
    )(partner_tiles.reshape(-1), points.reshape(tiles, TILE, features), targets)


def solution(mesh):
    return jax.shard_map(
        on_device,
        mesh=mesh,
        in_specs=(P(("group", "dev"), None), P(None, ("group", "dev")), P()),
        out_specs=(P(None, ("group", "dev")), P(None, ("group", "dev"))),
        check_vma=False,
    )
```

```python
import functools

import jax
import jax.numpy as jnp
from jax import lax
from jax.experimental import pallas as pl
from jax.experimental.pallas import tpu as pltpu
from jax.sharding import PartitionSpec as P

TILE = 256

length_scale = 3.9
noise_level = 1.0
coupling_weight = 0.5
value_weight = coupling_weight * 4.0 / length_scale**5
MESH = pl.DeviceIdType.MESH
NT = (((1,), (1,)), ((), ()))
NN = (((1,), (0,)), ((), ()))


def mxu(left, right, dims):
    return lax.dot_general(left, right, dims, preferred_element_type=jnp.float32)


def split_rows(values, ones):
    high = values.astype(jnp.bfloat16).astype(jnp.float32)
    pieces = [high, values - high]
    if ones:
        pieces += [jnp.ones_like(values), jnp.zeros_like(values)]
    return jnp.concatenate(pieces, axis=0).astype(jnp.bfloat16)


def merge_rows(summed, probes, ones):
    coupled = summed[0:probes] + summed[probes : 2 * probes]
    if ones:
        return jnp.concatenate([coupled, summed[2 * probes : 3 * probes]], axis=0)
    return coupled


def kernel(groups, devs, cap, probes, tiles,
           tab, pts, tgt, sol0, sol1, res0, res1,
           pin, outp, inp, kmat, kc, ncol, vec1, vin1, cvo1, cvi1, vec2, vin2, cvo2, cvi2,
           hout1, hin1, cho1, chi1, hout2, hin2, cho2, chi2,
           mown, mtile, mrem, mc, acc, acc2, deg, red1o, red1, red2o, red2,
           psend, precv, cpsend, cprecv, vsend, vrecv, cvsend, cvrecv,
           hsend, hrecv, chsend, chrecv, r1send, r1recv, r2send, r2recv):
    g = lax.axis_index("group")
    d = lax.axis_index("dev")
    par = lax.rem(d, 2)
    odd = par == 1
    even = par == 0
    peers = groups - 1
    cols = tiles * TILE

    def tile_id(owner, other, c):
        return tab[owner, d, other, c]

    def up(k):
        return lax.rem(g + k, groups)

    def down(k):
        return lax.rem(g + groups - k, groups)

    def cs(j):
        return slice(j * TILE, (j + 1) * TILE)

    @pl.loop(0, tiles)
    def _(i):
        wide = pts[i].astype(jnp.float32)
        ncol[i] = jnp.sum(wide * wide, axis=1, keepdims=True)

    for j in range(tiles):
        wide = pts[j].astype(jnp.float32)
        squares = wide * wide
        high = squares.astype(jnp.bfloat16)
        low = (squares - high.astype(jnp.float32)).astype(jnp.bfloat16)
        ones = jnp.ones((16, wide.shape[1]), jnp.bfloat16)
        sums = mxu(ones, high, NT) + mxu(ones, low, NT)
        vec1[0:probes, cs(j)] = tgt[:, cs(j)]
        vec1[probes : 2 * probes, cs(j)] = sums[0:probes]
        rows = split_rows(tgt[:, cs(j)], True)
        mown[:, cs(j)] = rows
        mtile[j] = rows
    for k in range(1, groups):
        for c in range(cap):
            named = tile_id(up(k), g, c)
            outp[k - 1, c] = pts[jnp.maximum(named, 0)]
            total = jnp.zeros((2 * probes, TILE), jnp.float32)
            for q in range(tiles):
                total = total + jnp.where(named == q, 1.0, 0.0) * vec1[:, cs(q)]
            cvo1[k - 1, :, cs(c)] = total

    barrier = pltpu.get_barrier_semaphore()
    for k in range(1, groups):
        pl.semaphore_signal(barrier, inc=1, device_id={"group": up(k)}, device_id_type=MESH)
    for k in range(1, devs):
        pl.semaphore_signal(barrier, inc=1, device_id={"dev": lax.rem(d + k, devs)}, device_id_type=MESH)
    pl.semaphore_wait(barrier, groups + devs - 2)

    def remote(src, dst, ssem, rsem, where):
        return pltpu.make_async_remote_copy(
            src_ref=src, dst_ref=dst, send_sem=ssem, recv_sem=rsem, device_id=where, device_id_type=MESH
        )

    has_next = d + 1 < devs
    far = jnp.where(odd, jnp.minimum(d + 2, devs - 1), jnp.maximum(d - 2, 0))
    has_far = jnp.logical_or(jnp.logical_and(odd, d + 2 < devs), jnp.logical_and(even, d >= 2))
    nxt = jnp.minimum(d + 1, devs - 1)
    has_first = jnp.logical_or(odd, d + 2 < devs)
    has_second = d >= 2
    first_owner = jnp.where(odd, jnp.maximum(d - 1, 0), jnp.minimum(d + 2, devs - 1))
    second_owner = jnp.where(odd, jnp.maximum(d - 2, 0), jnp.maximum(d - 1, 0))
    has_block = (has_first, has_second)
    block_owner = (first_owner, second_owner)
    block_slot = (1 - par, par)

    def vec_copy(r, which):
        src, dst = (vec1, vin1) if r == 0 else (vec2, vin2)
        return remote(src, dst.at[par], vsend.at[r, which], vrecv.at[r, par], {"dev": (nxt, far)[which]})

    def vec_in(r, block):
        src, dst = (vec1, vin1) if r == 0 else (vec2, vin2)
        return remote(src, dst.at[block], vsend.at[r, 0], vrecv.at[r, block], {"dev": nxt})

    def cvec(r, k):
        src, dst = (cvo1, cvi1) if r == 0 else (cvo2, cvi2)
        return remote(src.at[k - 1], dst.at[k - 1], cvsend.at[r, k - 1], cvrecv.at[r, k - 1], {"group": up(k)})

    def hand(r, block):
        src, dst = (hout1, hin1) if r == 0 else (hout2, hin2)
        slot = block_slot[block]
        return remote(src.at[block], dst.at[slot], hsend.at[r, block], hrecv.at[r, slot],
                      {"dev": block_owner[block]})

    def hand_in(r, slot):
        src, dst = (hout1, hin1) if r == 0 else (hout2, hin2)
        return remote(src.at[0], dst.at[slot], hsend.at[r, 0], hrecv.at[r, slot], {"dev": nxt})

    def chand(r, k):
        src, dst = (cho1, chi1) if r == 0 else (cho2, chi2)
        return remote(src.at[k - 1], dst.at[k - 1], chsend.at[r, k - 1], chrecv.at[r, k - 1], {"group": down(k)})

    def cpts(k):
        return remote(outp.at[k - 1], inp.at[k - 1], cpsend.at[k - 1], cprecv.at[k - 1], {"group": up(k)})

    far_pts = remote(pts, pin.at[par], psend.at[1], precv.at[par], {"dev": far})
    mate_pts = remote(pts, pin.at[0], psend.at[0], precv.at[0], {"dev": nxt})
    forward_pts = remote(pin.at[1], pin.at[1], psend.at[0], precv.at[1], {"dev": jnp.maximum(d - 1, 0)})

    def send_vectors(r):
        for which, cond in ((0, has_next), (1, has_far)):
            @pl.when(cond)
            def _():
                vec_copy(r, which).start()
        for k in range(1, groups):
            cvec(r, k).start()

    send_vectors(0)
    for k in range(1, groups):
        cpts(k).start()

    @pl.when(has_far)
    def _():
        far_pts.start()

    @pl.when(even)
    def _():
        mate_pts.start()

    def doubled(i):
        return pts[i] * jnp.asarray(-2.0, pts.dtype)

    def affinity(inner, norm_col, norm_row):
        dist_sq = jnp.maximum((norm_col + norm_row) + inner, 1e-30)
        near = jnp.maximum(length_scale - dist_sq * lax.rsqrt(dist_sq), 0.0)
        square = near * near
        return square * square * (1.25 * length_scale - near)

    def row_block(i, count, others, norm_row, finish):
        own = doubled(i)
        norm_col = jnp.broadcast_to(ncol[i], (TILE, TILE))
        inner = mxu(own, others(0), NT)
        for j in range(count):
            ahead = mxu(own, others(j + 1), NT) if j + 1 < count else None
            finish(j, affinity(inner, norm_col, norm_row(j)))
            inner = ahead

    fold = 2 if tiles % 2 == 0 else 1

    def row_loop(body):
        @pl.loop(0, tiles // fold)
        def _(step):
            for part in range(fold):
                body(step * fold + part)

    def own_rows(i):
        total = [jnp.zeros((4 * probes, TILE), jnp.float32)]

        def finish(j, value):
            value = value.astype(jnp.bfloat16)
            kmat[0, i, :, cs(j)] = value
            total[0] = total[0] + mxu(mown[:, cs(j)], value, NT)

        row_block(i, tiles, lambda j: pts[j], lambda j: vec1[probes : probes + 1, cs(j)], finish)
        acc[i] = total[0]

    row_loop(own_rows)

    def band(block):
        vec_in(0, block).wait_recv()
        for j in range(tiles):
            mrem[:, cs(j)] = split_rows(vin1[block, 0:probes, cs(j)], True)
        hout1[block] = jnp.zeros((2 * probes, cols), jnp.float32)

        def rows(i):
            total = [acc[i]]

            def finish(j, value):
                value = value.astype(jnp.bfloat16)
                kmat[1 + block, i, :, cs(j)] = value
                total[0] = total[0] + mxu(mrem[:, cs(j)], value, NT)
                hout1[block, :, cs(j)] += merge_rows(mxu(mtile[i], value, NN), probes, True)

            row_block(i, tiles, lambda j: pin[block, j], lambda j: vin1[block, probes : probes + 1, cs(j)], finish)
            acc[i] = total[0]

        row_loop(rows)
        hand(0, block).start()

    def cross(k):
        cvec(0, k).wait_recv()
        cpts(k).wait_recv()
        live = [jnp.where(tile_id(g, down(k), c) >= 0, 1.0, 0.0) for c in range(cap)]
        for c in range(cap):
            mc[k - 1, :, cs(c)] = split_rows(cvi1[k - 1, 0:probes, cs(c)], True)
        cho1[k - 1] = jnp.zeros((2 * probes, cap * TILE), jnp.float32)

        def rows(i):
            total = [acc[i]]

            def finish(c, value):
                value = (value * live[c]).astype(jnp.bfloat16)
                kc[k - 1, i, :, cs(c)] = value
                total[0] = total[0] + mxu(mc[k - 1, :, cs(c)], value, NT)
                cho1[k - 1, :, cs(c)] += merge_rows(mxu(mtile[i], value, NN), probes, True)

            row_block(i, cap, lambda c: inp[k - 1, c], lambda c: cvi1[k - 1, probes : probes + 1, cs(c)], finish)
            acc[i] = total[0]

        row_loop(rows)
        chand(0, k).start()

    @pl.when(has_first)
    def _():
        remote(pts, pin.at[0], psend.at[0], precv.at[0], {"dev": nxt}).wait_recv()
        band(0)

    cross(1)

    @pl.when(has_second)
    def _():
        remote(pts, pin.at[1], psend.at[0], precv.at[1], {"dev": nxt}).wait_recv()

        @pl.when(odd)
        def _():
            forward_pts.start()

        band(1)

    for k in range(2, groups):
        cross(k)

    def gather_backs(r, total):
        incoming, cross_in = (hin1, chi1) if r == 0 else (hin2, chi2)
        for k in range(1, groups):
            chand(r, k).wait_recv()
        for k in range(1, groups):
            for c in range(cap):
                named = tile_id(up(k), g, c)
                part = cross_in[k - 1, :, cs(c)]
                for q in range(tiles):
                    total[q] = total[q] + jnp.where(named == q, 1.0, 0.0) * part
        return total

    def wait_hands(r):
        for slot, cond in ((0, has_next), (1, has_far)):
            @pl.when(cond)
            def _():
                hand_in(r, slot).wait_recv()

    for slot, cond in ((0, has_next), (1, has_far)):
        @pl.when(jnp.logical_not(cond))
        def _():
            hin1[slot] = jnp.zeros((2 * probes, cols), jnp.float32)
            hin2[slot] = jnp.zeros((probes, cols), jnp.float32)

    wait_hands(0)
    sums = [merge_rows(acc[q], probes, True) + hin1[0, :, cs(q)] + hin1[1, :, cs(q)] for q in range(tiles)]
    sums = gather_backs(0, sums)
    for q in range(tiles):
        base = tgt[:, cs(q)]
        degree = sums[q][probes : 2 * probes]
        applied = noise_level * base + value_weight * (degree * base - sums[q][0:probes])
        vec2[:, cs(q)] = applied
        deg[:, cs(q)] = degree
    for k in range(1, groups):
        for c in range(cap):
            named = tile_id(up(k), g, c)
            total = jnp.zeros((probes, TILE), jnp.float32)
            for q in range(tiles):
                total = total + jnp.where(named == q, 1.0, 0.0) * vec2[:, cs(q)]
            cvo2[k - 1, :, cs(c)] = total
    send_vectors(1)

    for j in range(tiles):
        rows = split_rows(vec2[:, cs(j)], False)
        mown[0 : 2 * probes, cs(j)] = rows
    two = 2 * probes

    def whole(block):
        return kmat[block].reshape(cols, cols)

    acc2[...] = merge_rows(mxu(mown[0:two], whole(0), NT), probes, False)

    def merged(q):
        return acc2[:, cs(q)]

    quad_local = jnp.zeros((probes, 1), jnp.float32)
    for q in range(tiles):
        quad_local = quad_local + jnp.sum(vec2[:, cs(q)] * merged(q), axis=1, keepdims=True)

    def band_again(block):
        vec_in(1, block).wait_recv()
        for j in range(tiles):
            mrem[0:two, cs(j)] = split_rows(vin2[block, :, cs(j)], False)
        value = whole(1 + block)
        hout2[block] = merge_rows(mxu(mown[0:two], value, NN), probes, False)
        acc2[...] += merge_rows(mxu(mrem[0:two], value, NT), probes, False)
        hand(1, block).start()

    def cross_again(k):
        cvec(1, k).wait_recv()
        for c in range(cap):
            mc[k - 1, 0:two, cs(c)] = split_rows(cvi2[k - 1, :, cs(c)], False)
        value = kc[k - 1].reshape(cols, cap * TILE)
        cho2[k - 1] = merge_rows(mxu(mown[0:two], value, NN), probes, False)
        acc2[...] += merge_rows(mxu(mc[k - 1, 0:two], value, NT), probes, False)
        chand(1, k).start()

    for block in range(2):
        @pl.when(has_block[block])
        def _():
            band_again(block)

    for k in range(1, groups):
        cross_again(k)

    parts = [jnp.zeros((probes, 1), jnp.float32) for _ in range(5)]
    for q in range(tiles):
        base, applied, degree = tgt[:, cs(q)], vec2[:, cs(q)], deg[:, cs(q)]
        terms = (base * base, base * applied, applied * applied, degree * applied * applied, applied * merged(q))
        parts = [old + jnp.sum(term, axis=1, keepdims=True) for old, term in zip(parts, terms)]
    quad = 2.0 * parts[4] - quad_local
    curved = noise_level * parts[2] + value_weight * (parts[3] - quad)
    lane = lax.broadcasted_iota(jnp.int32, (probes, 128), 1)
    message = jnp.zeros((probes, 128), jnp.float32)
    for index, part in enumerate((parts[0], parts[1], parts[2], curved)):
        message = message + jnp.where(lane == index, part, 0.0)
    red1o[...] = message

    def reduce_one(k):
        return remote(red1o, red1.at[k - 1], r1send.at[k - 1], r1recv.at[k - 1], {"group": up(k)})

    def reduce_two(k):
        return remote(red2o, red2.at[k - 1], r2send.at[k - 1], r2recv.at[k - 1], {"dev": lax.rem(d + k, devs)})

    for k in range(1, groups):
        reduce_one(k).start()
    for k in range(1, groups):
        reduce_one(k).wait_recv()
    for k in range(1, groups):
        message = message + red1[k - 1]
    red2o[...] = message
    for k in range(1, devs):
        reduce_two(k).start()

    wait_hands(1)
    sums = [merged(q) + hin2[0, :, cs(q)] + hin2[1, :, cs(q)] for q in range(tiles)]
    sums = gather_backs(1, sums)
    for q in range(tiles):
        applied, degree = vec2[:, cs(q)], deg[:, cs(q)]
        res1[:, cs(q)] = noise_level * applied + value_weight * (degree * applied - sums[q])
    for k in range(1, devs):
        reduce_two(k).wait_recv()
    for k in range(1, devs):
        message = message + red2[k - 1]
    norm0, curv0, app_sq, app_curv = [
        jnp.sum(jnp.where(lane == index, message, 0.0), axis=1, keepdims=True) for index in range(4)
    ]
    step0 = norm0 / curv0
    norm1 = norm0 - 2.0 * step0 * curv0 + step0 * step0 * app_sq
    mix = 1.0 + norm1 / norm0
    curv1 = mix * mix * curv0 - 2.0 * mix * step0 * app_sq + step0 * step0 * app_curv
    step1 = norm1 / curv1
    for q in range(tiles):
        base, applied, twice = tgt[:, cs(q)], vec2[:, cs(q)], res1[:, cs(q)]
        sol0[:, cs(q)] = step0 * base
        sol1[:, cs(q)] = step1 * (mix * base - step0 * applied)
        res0[:, cs(q)] = base - step0 * applied
        res1[:, cs(q)] = step1 * (mix * applied - step0 * twice)

    for r in range(2):
        for which, cond in ((0, has_next), (1, has_far)):
            @pl.when(cond)
            def _():
                vec_copy(r, which).wait_send()
        for block in range(2):
            @pl.when(has_block[block])
            def _():
                hand(r, block).wait_send()
        for k in range(1, groups):
            cvec(r, k).wait_send()
            chand(r, k).wait_send()
    for k in range(1, groups):
        cpts(k).wait_send()
        reduce_one(k).wait_send()
    for k in range(1, devs):
        reduce_two(k).wait_send()

    @pl.when(has_far)
    def _():
        far_pts.wait_send()

    @pl.when(even)
    def _():
        mate_pts.wait_send()

    @pl.when(jnp.logical_and(odd, has_second))
    def _():
        forward_pts.wait_send()


def on_device(points, targets, partner_tiles):
    groups, devs, _, cap = partner_tiles.shape
    rows, features = points.shape
    tiles = rows // TILE
    probes = targets.shape[0]
    peers = groups - 1
    f32, bf16 = jnp.float32, jnp.bfloat16
    v = pltpu.VMEM
    dma = pltpu.SemaphoreType.DMA
    wide = cap * TILE
    two = 2 * probes
    scratch = [
        v((2, tiles, TILE, features), bf16),
        v((peers, cap, TILE, features), bf16),
        v((peers, cap, TILE, features), bf16),
        v((3, tiles, TILE, rows), bf16),
        v((peers, tiles, TILE, wide), bf16),
        v((tiles, TILE, 1), f32),
        v((two, rows), f32),
        v((2, two, rows), f32),
        v((peers, two, wide), f32),
        v((peers, two, wide), f32),
        v((probes, rows), f32),
        v((2, probes, rows), f32),
        v((peers, probes, wide), f32),
        v((peers, probes, wide), f32),
        v((2, two, rows), f32),
        v((2, two, rows), f32),
        v((peers, two, wide), f32),
        v((peers, two, wide), f32),
        v((2, probes, rows), f32),
        v((2, probes, rows), f32),
        v((peers, probes, wide), f32),
        v((peers, probes, wide), f32),
        v((2 * two, rows), bf16),
        v((tiles, 2 * two, TILE), bf16),
        v((2 * two, rows), bf16),
        v((peers, 2 * two, wide), bf16),
        v((tiles, 2 * two, TILE), f32),
        v((probes, rows), f32),
        v((probes, rows), f32),
        v((probes, 128), f32),
        v((peers, probes, 128), f32),
        v((probes, 128), f32),
        v((devs - 1, probes, 128), f32),
        dma((2,)), dma((2,)), dma((peers,)), dma((peers,)),
        dma((2, 2)), dma((2, 2)), dma((2, peers)), dma((2, peers)),
        dma((2, 2)), dma((2, 2)), dma((2, peers)), dma((2, peers)),
        dma((peers,)), dma((peers,)), dma((devs - 1,)), dma((devs - 1,)),
    ]
    pairs = rows * rows * 3 + rows * wide * peers
    sol0, sol1, res0, res1 = pl.pallas_call(
        functools.partial(kernel, groups, devs, cap, probes, tiles),
        out_shape=(jax.ShapeDtypeStruct(targets.shape, f32),) * 4,
        in_specs=[
            pl.BlockSpec(memory_space=pltpu.SMEM),
            pl.BlockSpec(memory_space=pltpu.VMEM),
            pl.BlockSpec(memory_space=pltpu.VMEM),
        ],
        out_specs=(pl.BlockSpec(memory_space=pltpu.VMEM),) * 4,
        scratch_shapes=scratch,
        compiler_params=pltpu.CompilerParams(
            collective_id=0, has_side_effects=True, vmem_limit_bytes=56 * 1024 * 1024
        ),
        cost_estimate=pl.CostEstimate(flops=2 * features * pairs, bytes_accessed=rows * features * 2, transcendentals=pairs),
        name="graph_cg",
    )(partner_tiles, points.reshape(tiles, TILE, features), targets)
    return (sol0 + sol1, res0 - res1)


def solution(mesh):
    return jax.shard_map(
        on_device,
        mesh=mesh,
        in_specs=(P(("group", "dev"), None), P(None, ("group", "dev")), P()),
        out_specs=(P(None, ("group", "dev")), P(None, ("group", "dev"))),
        check_vma=False,
    )
```

```python
import functools

import jax
import jax.numpy as jnp
from jax import lax
from jax.experimental import pallas as pl
from jax.experimental.pallas import tpu as pltpu
from jax.sharding import PartitionSpec as P

TILE = 256

length_scale = 3.9
noise_level = 1.0
coupling_weight = 0.5
value_weight = coupling_weight * 4.0 / length_scale**5
MESH = pl.DeviceIdType.MESH
NT = (((1,), (1,)), ((), ()))
NN = (((1,), (0,)), ((), ()))


def mxu(left, right, dims):
    return lax.dot_general(left, right, dims, preferred_element_type=jnp.float32)


def split_rows(values, ones):
    high = values.astype(jnp.bfloat16).astype(jnp.float32)
    pieces = [high, values - high]
    if ones:
        pieces += [jnp.ones_like(values), jnp.zeros_like(values)]
    return jnp.concatenate(pieces, axis=0).astype(jnp.bfloat16)


def merge_rows(summed, probes, ones):
    coupled = summed[0:probes] + summed[probes : 2 * probes]
    if ones:
        return jnp.concatenate([coupled, summed[2 * probes : 3 * probes]], axis=0)
    return coupled


def kernel(groups, devs, cap, probes, tiles,
           tab, pts, tgt, sol0, sol1, res1,
           pin, outp, inp, kmat, kc, ncol, twin, vec1, vin1, cvo1, cvi1, vec2, vin2, cvo2, cvi2,
           hout1, hin1, cho1, chi1, hout2, hin2, cho2, chi2,
           mown, mtile, mrem, mc, acc, acc2, deg, red1o, red1, red2o, red2,
           psend, precv, cpsend, cprecv, vsend, vrecv, cvsend, cvrecv,
           hsend, hrecv, chsend, chrecv, r1send, r1recv, r2send, r2recv):
    g = lax.axis_index("group")
    d = lax.axis_index("dev")
    par = lax.rem(d, 2)
    odd = par == 1
    even = par == 0
    peers = groups - 1
    cols = tiles * TILE

    def tile_id(owner, other, c):
        return tab[owner, other, c, d]

    def up(k):
        return lax.rem(g + k, groups)

    def down(k):
        return lax.rem(g + groups - k, groups)

    def cs(j):
        return slice(j * TILE, (j + 1) * TILE)

    barrier = pltpu.get_barrier_semaphore()
    for k in range(1, groups):
        pl.semaphore_signal(barrier, inc=1, device_id={"group": up(k)}, device_id_type=MESH)
    for k in range(1, devs):
        pl.semaphore_signal(barrier, inc=1, device_id={"dev": lax.rem(d + k, devs)}, device_id_type=MESH)

    @pl.loop(0, tiles)
    def _(i):
        wide = pts[i].astype(jnp.float32)
        twin[i] = pts[i] * jnp.asarray(-2.0, pts.dtype)
        ncol[i] = jnp.sum(wide * wide, axis=1, keepdims=True)

    for j in range(tiles):
        wide = pts[j].astype(jnp.float32)
        squares = wide * wide
        high = squares.astype(jnp.bfloat16)
        low = (squares - high.astype(jnp.float32)).astype(jnp.bfloat16)
        ones = jnp.ones((16, wide.shape[1]), jnp.bfloat16)
        sums = mxu(ones, high, NT) + mxu(ones, low, NT)
        vec1[0:probes, cs(j)] = tgt[:, cs(j)]
        vec1[probes : 2 * probes, cs(j)] = sums[0:probes]
        rows = split_rows(tgt[:, cs(j)], True)
        mown[:, cs(j)] = rows
        mtile[j] = rows
    for k in range(1, groups):
        for c in range(cap):
            named = tile_id(up(k), g, c)
            outp[k - 1, c] = pts[jnp.maximum(named, 0)]
            total = jnp.zeros((2 * probes, TILE), jnp.float32)
            for q in range(tiles):
                total = total + jnp.where(named == q, 1.0, 0.0) * vec1[:, cs(q)]
            cvo1[k - 1, :, cs(c)] = total

    pl.semaphore_wait(barrier, groups + devs - 2)

    def remote(src, dst, ssem, rsem, where):
        return pltpu.make_async_remote_copy(
            src_ref=src, dst_ref=dst, send_sem=ssem, recv_sem=rsem, device_id=where, device_id_type=MESH
        )

    has_next = d + 1 < devs
    far = jnp.where(odd, jnp.minimum(d + 2, devs - 1), jnp.maximum(d - 2, 0))
    has_far = jnp.logical_or(jnp.logical_and(odd, d + 2 < devs), jnp.logical_and(even, d >= 2))
    nxt = jnp.minimum(d + 1, devs - 1)
    has_first = jnp.logical_or(odd, d + 2 < devs)
    has_second = d >= 2
    first_owner = jnp.where(odd, jnp.maximum(d - 1, 0), jnp.minimum(d + 2, devs - 1))
    second_owner = jnp.where(odd, jnp.maximum(d - 2, 0), jnp.maximum(d - 1, 0))
    has_block = (has_first, has_second)
    block_owner = (first_owner, second_owner)
    block_slot = (1 - par, par)

    def vec_copy(r, which):
        src, dst = (vec1, vin1) if r == 0 else (vec2, vin2)
        return remote(src, dst.at[par], vsend.at[r, which], vrecv.at[r, par], {"dev": (nxt, far)[which]})

    def vec_in(r, block):
        src, dst = (vec1, vin1) if r == 0 else (vec2, vin2)
        return remote(src, dst.at[block], vsend.at[r, 0], vrecv.at[r, block], {"dev": nxt})

    def cvec(r, k):
        src, dst = (cvo1, cvi1) if r == 0 else (cvo2, cvi2)
        return remote(src.at[k - 1], dst.at[k - 1], cvsend.at[r, k - 1], cvrecv.at[r, k - 1], {"group": up(k)})

    def hand(r, block):
        src, dst = (hout1, hin1) if r == 0 else (hout2, hin2)
        slot = block_slot[block]
        return remote(src.at[block], dst.at[slot], hsend.at[r, block], hrecv.at[r, slot],
                      {"dev": block_owner[block]})

    def hand_in(r, slot):
        src, dst = (hout1, hin1) if r == 0 else (hout2, hin2)
        return remote(src.at[0], dst.at[slot], hsend.at[r, 0], hrecv.at[r, slot], {"dev": nxt})

    def chand(r, k):
        src, dst = (cho1, chi1) if r == 0 else (cho2, chi2)
        return remote(src.at[k - 1], dst.at[k - 1], chsend.at[r, k - 1], chrecv.at[r, k - 1], {"group": down(k)})

    def cpts(k):
        return remote(outp.at[k - 1], inp.at[k - 1], cpsend.at[k - 1], cprecv.at[k - 1], {"group": up(k)})

    fold = 2 if tiles % 2 == 0 else 1
    chunks = tiles // fold

    def piece(s):
        return pl.ds(s * fold, fold)

    def far_pts(s):
        return remote(pts.at[piece(s)], pin.at[par, piece(s)], psend.at[1, s], precv.at[par, s], {"dev": far})

    def mate_pts(s):
        return remote(pts.at[piece(s)], pin.at[0, piece(s)], psend.at[0, s], precv.at[0, s], {"dev": nxt})

    def forward_pts(s):
        return remote(pin.at[1, piece(s)], pin.at[1, piece(s)], psend.at[0, s], precv.at[1, s],
                      {"dev": jnp.maximum(d - 1, 0)})

    def pts_in(block, s):
        return remote(pts.at[piece(s)], pin.at[block, piece(s)], psend.at[0, s], precv.at[block, s], {"dev": nxt})

    def send_vectors(r):
        for which, cond in ((0, has_next), (1, has_far)):
            @pl.when(cond)
            def _():
                vec_copy(r, which).start()
        for k in range(1, groups):
            cvec(r, k).start()

    send_vectors(0)
    cpts(1).start()

    @pl.when(even)
    def _():
        for s in range(chunks):
            mate_pts(s).start()

    @pl.when(has_far)
    def _():
        for s in range(chunks):
            far_pts(s).start()

    for k in range(2, groups):
        cpts(k).start()

    def affinity(inner, norm_col, norm_row):
        dist_sq = jnp.maximum((norm_col + norm_row) + inner, 1e-30)
        near = jnp.maximum(length_scale - dist_sq * lax.rsqrt(dist_sq), 0.0)
        square = near * near
        return square * square * (1.25 * length_scale - near)

    def row_block(i, count, others, norm_row, finish):
        own = twin[i]
        norm_col = jnp.broadcast_to(ncol[i], (TILE, TILE))
        inner = mxu(own, others(0), NT)
        for j in range(count):
            ahead = mxu(own, others(j + 1), NT) if j + 1 < count else None
            finish(j, affinity(inner, norm_col, norm_row(j)))
            inner = ahead

    def row_loop(body):
        @pl.loop(0, tiles // fold)
        def _(step):
            for inner in range(fold):
                body(step * fold + inner)

    def own_rows(i):
        total = [jnp.zeros((4 * probes, TILE), jnp.float32)]

        def finish(j, value):
            value = value.astype(jnp.bfloat16)
            kmat[0, i, :, cs(j)] = value
            total[0] = total[0] + mxu(mown[:, cs(j)], value, NT)

        row_block(i, tiles, lambda j: pts[j], lambda j: vec1[probes : probes + 1, cs(j)], finish)
        acc[i] = total[0]

    row_loop(own_rows)

    def band(block):
        vec_in(0, block).wait_recv()

        def column(j):
            span = pl.ds(pl.multiple_of(j * TILE, TILE), TILE)
            theirs = split_rows(vin1[block, 0:probes, span], True)
            norm_row = vin1[block, probes : probes + 1, span]
            total = jnp.zeros((4 * probes, TILE), jnp.float32)
            inner = mxu(twin[0], pin[block, j], NT)
            for i in range(tiles):
                ahead = mxu(twin[i + 1], pin[block, j], NT) if i + 1 < tiles else None
                value = affinity(inner, ncol[i], norm_row).astype(jnp.bfloat16)
                kmat[1 + block, i, :, span] = value
                acc[i] += mxu(theirs, value, NT)
                total = total + mxu(mtile[i], value, NN)
                inner = ahead
            hout1[block, :, span] = merge_rows(total, probes, True)

        @pl.loop(0, chunks)
        def _(s):
            pts_in(block, s).wait_recv()
            if block == 1:
                @pl.when(odd)
                def _():
                    forward_pts(s).start()

            for inner in range(fold):
                column(s * fold + inner)

        hand(0, block).start()

    def cross(k):
        cvec(0, k).wait_recv()
        cpts(k).wait_recv()
        live = [jnp.where(tile_id(g, down(k), c) >= 0, 1.0, 0.0) for c in range(cap)]
        for c in range(cap):
            mc[k - 1, :, cs(c)] = split_rows(cvi1[k - 1, 0:probes, cs(c)], True)
        cho1[k - 1] = jnp.zeros((2 * probes, cap * TILE), jnp.float32)

        def rows(i):
            total = [acc[i]]

            def finish(c, value):
                value = (value * live[c]).astype(jnp.bfloat16)
                kc[k - 1, i, :, cs(c)] = value
                total[0] = total[0] + mxu(mc[k - 1, :, cs(c)], value, NT)
                cho1[k - 1, :, cs(c)] += merge_rows(mxu(mtile[i], value, NN), probes, True)

            row_block(i, cap, lambda c: inp[k - 1, c], lambda c: cvi1[k - 1, probes : probes + 1, cs(c)], finish)
            acc[i] = total[0]

        row_loop(rows)
        chand(0, k).start()

    @pl.when(odd)
    def _():
        band(0)

    cross(1)

    @pl.when(jnp.logical_and(even, has_first))
    def _():
        band(0)

    @pl.when(has_second)
    def _():
        band(1)

    for k in range(2, groups):
        cross(k)

    def gather_backs(r, total):
        incoming, cross_in = (hin1, chi1) if r == 0 else (hin2, chi2)
        for k in range(1, groups):
            chand(r, k).wait_recv()
        for k in range(1, groups):
            for c in range(cap):
                named = tile_id(up(k), g, c)
                part = cross_in[k - 1, :, cs(c)]
                for q in range(tiles):
                    total[q] = total[q] + jnp.where(named == q, 1.0, 0.0) * part
        return total

    def wait_hands(r):
        for slot, cond in ((0, has_next), (1, has_far)):
            @pl.when(cond)
            def _():
                hand_in(r, slot).wait_recv()

    for slot, cond in ((0, has_next), (1, has_far)):
        @pl.when(jnp.logical_not(cond))
        def _():
            hin1[slot] = jnp.zeros((2 * probes, cols), jnp.float32)
            hin2[slot] = jnp.zeros((probes, cols), jnp.float32)

    wait_hands(0)
    sums = [merge_rows(acc[q], probes, True) + hin1[0, :, cs(q)] + hin1[1, :, cs(q)] for q in range(tiles)]
    sums = gather_backs(0, sums)
    for q in range(tiles):
        base = tgt[:, cs(q)]
        degree = sums[q][probes : 2 * probes]
        applied = noise_level * base + value_weight * (degree * base - sums[q][0:probes])
        vec2[:, cs(q)] = applied
        deg[:, cs(q)] = degree
    for k in range(1, groups):
        for c in range(cap):
            named = tile_id(up(k), g, c)
            total = jnp.zeros((probes, TILE), jnp.float32)
            for q in range(tiles):
                total = total + jnp.where(named == q, 1.0, 0.0) * vec2[:, cs(q)]
            cvo2[k - 1, :, cs(c)] = total
    send_vectors(1)

    for j in range(tiles):
        rows = split_rows(vec2[:, cs(j)], False)
        mown[0 : 2 * probes, cs(j)] = rows
    two = 2 * probes

    def whole(block):
        return kmat[block].reshape(cols, cols)

    acc2[...] = merge_rows(mxu(mown[0:two], whole(0), NT), probes, False)

    def merged(q):
        return acc2[:, cs(q)]

    quad_local = jnp.zeros((probes, 1), jnp.float32)
    for q in range(tiles):
        quad_local = quad_local + jnp.sum(vec2[:, cs(q)] * merged(q), axis=1, keepdims=True)

    def band_again(block):
        vec_in(1, block).wait_recv()
        for j in range(tiles):
            mrem[0:two, cs(j)] = split_rows(vin2[block, :, cs(j)], False)
        value = whole(1 + block)
        hout2[block] = merge_rows(mxu(mown[0:two], value, NN), probes, False)
        acc2[...] += merge_rows(mxu(mrem[0:two], value, NT), probes, False)
        hand(1, block).start()

    def cross_again(k):
        cvec(1, k).wait_recv()
        for c in range(cap):
            mc[k - 1, 0:two, cs(c)] = split_rows(cvi2[k - 1, :, cs(c)], False)
        value = kc[k - 1].reshape(cols, cap * TILE)
        cho2[k - 1] = merge_rows(mxu(mown[0:two], value, NN), probes, False)
        acc2[...] += merge_rows(mxu(mc[k - 1, 0:two], value, NT), probes, False)
        chand(1, k).start()

    for block in range(2):
        @pl.when(has_block[block])
        def _():
            band_again(block)

    for k in range(1, groups):
        cross_again(k)

    parts = [jnp.zeros((probes, 1), jnp.float32) for _ in range(5)]
    for q in range(tiles):
        base, applied, degree = tgt[:, cs(q)], vec2[:, cs(q)], deg[:, cs(q)]
        terms = (base * base, base * applied, applied * applied, degree * applied * applied, applied * merged(q))
        parts = [old + jnp.sum(term, axis=1, keepdims=True) for old, term in zip(parts, terms)]
    quad = 2.0 * parts[4] - quad_local
    curved = noise_level * parts[2] + value_weight * (parts[3] - quad)
    lane = lax.broadcasted_iota(jnp.int32, (probes, 128), 1)
    message = jnp.zeros((probes, 128), jnp.float32)
    for index, part in enumerate((parts[0], parts[1], parts[2], curved)):
        message = message + jnp.where(lane == index, part, 0.0)
    red1o[...] = message

    def reduce_one(k):
        return remote(red1o, red1.at[k - 1], r1send.at[k - 1], r1recv.at[k - 1], {"group": up(k)})

    def reduce_two(k):
        return remote(red2o, red2.at[k - 1], r2send.at[k - 1], r2recv.at[k - 1], {"dev": lax.rem(d + k, devs)})

    for k in range(1, groups):
        reduce_one(k).start()
    for k in range(1, groups):
        reduce_one(k).wait_recv()
    for k in range(1, groups):
        message = message + red1[k - 1]
    red2o[...] = message
    for k in range(1, devs):
        reduce_two(k).start()

    wait_hands(1)
    sums = [merged(q) + hin2[0, :, cs(q)] + hin2[1, :, cs(q)] for q in range(tiles)]
    sums = gather_backs(1, sums)
    for q in range(tiles):
        applied, degree = vec2[:, cs(q)], deg[:, cs(q)]
        res1[:, cs(q)] = noise_level * applied + value_weight * (degree * applied - sums[q])
    for k in range(1, devs):
        reduce_two(k).wait_recv()
    for k in range(1, devs):
        message = message + red2[k - 1]
    norm0, curv0, app_sq, app_curv = [
        jnp.sum(jnp.where(lane == index, message, 0.0), axis=1, keepdims=True) for index in range(4)
    ]
    step0 = norm0 / curv0
    norm1 = norm0 - 2.0 * step0 * curv0 + step0 * step0 * app_sq
    mix = 1.0 + norm1 / norm0
    curv1 = mix * mix * curv0 - 2.0 * mix * step0 * app_sq + step0 * step0 * app_curv
    step1 = norm1 / curv1
    for q in range(tiles):
        base, applied, twice = tgt[:, cs(q)], vec2[:, cs(q)], res1[:, cs(q)]
        sol0[:, cs(q)] = step0 * base
        sol1[:, cs(q)] = step1 * (mix * base - step0 * applied)
        left = (base - step0 * applied) - step1 * (mix * applied - step0 * twice)
        res1[:, cs(q)] = left - step0 * base

    for r in range(2):
        for which, cond in ((0, has_next), (1, has_far)):
            @pl.when(cond)
            def _():
                vec_copy(r, which).wait_send()
        for block in range(2):
            @pl.when(has_block[block])
            def _():
                hand(r, block).wait_send()
        for k in range(1, groups):
            cvec(r, k).wait_send()
            chand(r, k).wait_send()
    for k in range(1, groups):
        cpts(k).wait_send()
        reduce_one(k).wait_send()
    for k in range(1, devs):
        reduce_two(k).wait_send()

    @pl.when(has_far)
    def _():
        for s in range(chunks):
            far_pts(s).wait_send()

    @pl.when(even)
    def _():
        for s in range(chunks):
            mate_pts(s).wait_send()

    @pl.when(jnp.logical_and(odd, has_second))
    def _():
        for s in range(chunks):
            forward_pts(s).wait_send()


def on_device(points, targets, partner_tiles):
    groups, devs, _, cap = partner_tiles.shape
    rows, features = points.shape
    tiles = rows // TILE
    probes = targets.shape[0]
    peers = groups - 1
    f32, bf16 = jnp.float32, jnp.bfloat16
    v = pltpu.VMEM
    dma = pltpu.SemaphoreType.DMA
    wide = cap * TILE
    two = 2 * probes
    scratch = [
        v((2, tiles, TILE, features), bf16),
        v((peers, cap, TILE, features), bf16),
        v((peers, cap, TILE, features), bf16),
        v((3, tiles, TILE, rows), bf16),
        v((peers, tiles, TILE, wide), bf16),
        v((tiles, TILE, 1), f32),
        v((tiles, TILE, features), bf16),
        v((two, rows), f32),
        v((2, two, rows), f32),
        v((peers, two, wide), f32),
        v((peers, two, wide), f32),
        v((probes, rows), f32),
        v((2, probes, rows), f32),
        v((peers, probes, wide), f32),
        v((peers, probes, wide), f32),
        v((2, two, rows), f32),
        v((2, two, rows), f32),
        v((peers, two, wide), f32),
        v((peers, two, wide), f32),
        v((2, probes, rows), f32),
        v((2, probes, rows), f32),
        v((peers, probes, wide), f32),
        v((peers, probes, wide), f32),
        v((2 * two, rows), bf16),
        v((tiles, 2 * two, TILE), bf16),
        v((2 * two, rows), bf16),
        v((peers, 2 * two, wide), bf16),
        v((tiles, 2 * two, TILE), f32),
        v((probes, rows), f32),
        v((probes, rows), f32),
        v((probes, 128), f32),
        v((peers, probes, 128), f32),
        v((probes, 128), f32),
        v((devs - 1, probes, 128), f32),
        dma((2, tiles)), dma((2, tiles)), dma((peers,)), dma((peers,)),
        dma((2, 2)), dma((2, 2)), dma((2, peers)), dma((2, peers)),
        dma((2, 2)), dma((2, 2)), dma((2, peers)), dma((2, peers)),
        dma((peers,)), dma((peers,)), dma((devs - 1,)), dma((devs - 1,)),
    ]
    pairs = rows * rows * 3 + rows * wide * peers
    sol0, sol1, res1 = pl.pallas_call(
        functools.partial(kernel, groups, devs, cap, probes, tiles),
        out_shape=(jax.ShapeDtypeStruct(targets.shape, f32),) * 3,
        in_specs=[
            pl.BlockSpec(memory_space=pltpu.SMEM),
            pl.BlockSpec(memory_space=pltpu.VMEM),
            pl.BlockSpec(memory_space=pltpu.VMEM),
        ],
        out_specs=(pl.BlockSpec(memory_space=pltpu.VMEM),) * 3,
        scratch_shapes=scratch,
        compiler_params=pltpu.CompilerParams(
            collective_id=0, has_side_effects=True, vmem_limit_bytes=56 * 1024 * 1024
        ),
        cost_estimate=pl.CostEstimate(flops=2 * features * pairs, bytes_accessed=rows * features * 2, transcendentals=pairs),
        name="graph_cg",
    )(jnp.transpose(partner_tiles, (0, 2, 3, 1)), points.reshape(tiles, TILE, features), targets)
    return (sol0 + sol1, sol0 + res1)


def solution(mesh):
    return jax.shard_map(
        on_device,
        mesh=mesh,
        in_specs=(P(("group", "dev"), None), P(None, ("group", "dev")), P()),
        out_specs=(P(None, ("group", "dev")), P(None, ("group", "dev"))),
        check_vma=False,
    )
```

```python
import functools

import jax
import jax.numpy as jnp
from jax import lax
from jax.experimental import pallas as pl
from jax.experimental.pallas import tpu as pltpu
from jax.sharding import PartitionSpec as P

TILE = 256

length_scale = 3.9
noise_level = 1.0
coupling_weight = 0.5
value_weight = coupling_weight * 4.0 / length_scale**5
PIECE = 32
MESH = pl.DeviceIdType.MESH
NT = (((1,), (1,)), ((), ()))
NN = (((1,), (0,)), ((), ()))


def mxu(left, right, dims):
    return lax.dot_general(left, right, dims, preferred_element_type=jnp.float32)


def split_rows(values, ones):
    high = values.astype(jnp.bfloat16).astype(jnp.float32)
    pieces = [high, values - high]
    if ones:
        pieces += [jnp.ones_like(values), jnp.zeros_like(values)]
    return jnp.concatenate(pieces, axis=0).astype(jnp.bfloat16)


def merge_rows(summed, probes, ones):
    coupled = summed[0:probes] + summed[probes : 2 * probes]
    if ones:
        return jnp.concatenate([coupled, summed[2 * probes : 3 * probes]], axis=0)
    return coupled


def kernel(groups, devs, cap, probes, tiles,
           tab, pts, tgt, sol0, sol1, res1,
           pin, outp, inp, kmat, kc, ncol, twin, grama, gramb, vec1, vin1, cvo1, cvi1, vec2, vin2, cvo2, cvi2,
           hout1, hin1, cho1, chi1, hout2, hin2, cho2, chi2,
           mown, mrem, mc, acc, acc2, deg, red1o, red1, red2o, red2,
           psend, precv, cpsend, cprecv, vsend, vrecv, cvsend, cvrecv,
           hsend, hrecv, chsend, chrecv, r1send, r1recv, r2send, r2recv):
    g = lax.axis_index("group")
    d = lax.axis_index("dev")
    par = lax.rem(d, 2)
    odd = par == 1
    even = par == 0
    peers = groups - 1
    cols = tiles * TILE

    def tile_id(owner, other, c):
        return tab[owner, other, c, d]

    def up(k):
        return lax.rem(g + k, groups)

    def down(k):
        return lax.rem(g + groups - k, groups)

    def cs(j):
        return slice(j * TILE, (j + 1) * TILE)

    barrier = pltpu.get_barrier_semaphore()
    for k in range(1, groups):
        pl.semaphore_signal(barrier, inc=1, device_id={"group": up(k)}, device_id_type=MESH)
    for k in range(1, devs):
        pl.semaphore_signal(barrier, inc=1, device_id={"dev": lax.rem(d + k, devs)}, device_id_type=MESH)

    @pl.loop(0, tiles)
    def _(i):
        wide = pts[i].astype(jnp.float32)
        twin[i] = pts[i] * jnp.asarray(-2.0, pts.dtype)
        ncol[i] = jnp.sum(wide * wide, axis=1, keepdims=True)

    for j in range(tiles):
        wide = pts[j].astype(jnp.float32)
        squares = wide * wide
        high = squares.astype(jnp.bfloat16)
        low = (squares - high.astype(jnp.float32)).astype(jnp.bfloat16)
        ones = jnp.ones((16, wide.shape[1]), jnp.bfloat16)
        sums = mxu(ones, high, NT) + mxu(ones, low, NT)
        vec1[0:probes, cs(j)] = tgt[:, cs(j)]
        vec1[probes : 2 * probes, cs(j)] = sums[0:probes]
        rows = split_rows(tgt[:, cs(j)], True)
        mown[:, cs(j)] = rows
    for k in range(1, groups):
        for c in range(cap):
            named = tile_id(up(k), g, c)
            outp[k - 1, c] = pts[jnp.maximum(named, 0)]
            total = jnp.zeros((2 * probes, TILE), jnp.float32)
            for q in range(tiles):
                total = total + jnp.where(named == q, 1.0, 0.0) * vec1[:, cs(q)]
            cvo1[k - 1, :, cs(c)] = total

    pl.semaphore_wait(barrier, groups + devs - 2)

    def remote(src, dst, ssem, rsem, where):
        return pltpu.make_async_remote_copy(
            src_ref=src, dst_ref=dst, send_sem=ssem, recv_sem=rsem, device_id=where, device_id_type=MESH
        )

    has_next = d + 1 < devs
    far = jnp.where(odd, jnp.minimum(d + 2, devs - 1), jnp.maximum(d - 2, 0))
    has_far = jnp.logical_or(jnp.logical_and(odd, d + 2 < devs), jnp.logical_and(even, d >= 2))
    nxt = jnp.minimum(d + 1, devs - 1)
    has_first = jnp.logical_or(odd, d + 2 < devs)
    has_second = d >= 2
    first_owner = jnp.where(odd, jnp.maximum(d - 1, 0), jnp.minimum(d + 2, devs - 1))
    second_owner = jnp.where(odd, jnp.maximum(d - 2, 0), jnp.maximum(d - 1, 0))
    has_block = (has_first, has_second)
    block_owner = (first_owner, second_owner)
    block_slot = (1 - par, par)

    def vec_copy(r, which):
        src, dst = (vec1, vin1) if r == 0 else (vec2, vin2)
        return remote(src, dst.at[par], vsend.at[r, which], vrecv.at[r, par], {"dev": (nxt, far)[which]})

    def vec_in(r, block):
        src, dst = (vec1, vin1) if r == 0 else (vec2, vin2)
        return remote(src, dst.at[block], vsend.at[r, 0], vrecv.at[r, block], {"dev": nxt})

    def cvec(r, k):
        src, dst = (cvo1, cvi1) if r == 0 else (cvo2, cvi2)
        return remote(src.at[k - 1], dst.at[k - 1], cvsend.at[r, k - 1], cvrecv.at[r, k - 1], {"group": up(k)})

    def hand(r, block):
        src, dst = (hout1, hin1) if r == 0 else (hout2, hin2)
        slot = block_slot[block]
        return remote(src.at[block], dst.at[slot], hsend.at[r, block], hrecv.at[r, slot],
                      {"dev": block_owner[block]})

    def hand_in(r, slot):
        src, dst = (hout1, hin1) if r == 0 else (hout2, hin2)
        return remote(src.at[0], dst.at[slot], hsend.at[r, 0], hrecv.at[r, slot], {"dev": nxt})

    def chand(r, k):
        src, dst = (cho1, chi1) if r == 0 else (cho2, chi2)
        return remote(src.at[k - 1], dst.at[k - 1], chsend.at[r, k - 1], chrecv.at[r, k - 1], {"group": down(k)})

    def cpts(k):
        return remote(outp.at[k - 1], inp.at[k - 1], cpsend.at[k - 1], cprecv.at[k - 1], {"group": up(k)})

    fold = 2 if tiles % 2 == 0 else 1
    chunks = tiles // fold

    def piece(s):
        return pl.ds(s * fold, fold)

    def far_pts(s):
        return remote(pts.at[piece(s)], pin.at[par, piece(s)], psend.at[1, s], precv.at[par, s], {"dev": far})

    def mate_pts(s):
        return remote(pts.at[piece(s)], pin.at[0, piece(s)], psend.at[0, s], precv.at[0, s], {"dev": nxt})

    def forward_pts(s):
        return remote(pin.at[1, piece(s)], pin.at[1, piece(s)], psend.at[0, s], precv.at[1, s],
                      {"dev": jnp.maximum(d - 1, 0)})

    def pts_in(block, s):
        return remote(pts.at[piece(s)], pin.at[block, piece(s)], psend.at[0, s], precv.at[block, s], {"dev": nxt})

    def send_vectors(r):
        for which, cond in ((0, has_next), (1, has_far)):
            @pl.when(cond)
            def _():
                vec_copy(r, which).start()
        for k in range(1, groups):
            cvec(r, k).start()

    send_vectors(0)
    cpts(1).start()

    @pl.when(even)
    def _():
        for s in range(chunks):
            mate_pts(s).start()

    @pl.when(has_far)
    def _():
        for s in range(chunks):
            far_pts(s).start()

    for k in range(2, groups):
        cpts(k).start()

    def affinity(inner, norm_col, norm_row):
        dist_sq = jnp.maximum((norm_col + norm_row) + inner, 1e-30)
        near = jnp.maximum(length_scale - dist_sq * lax.rsqrt(dist_sq), 0.0)
        square = near * near
        return square * square * (1.25 * length_scale - near)

    def panels(other, theirs, norm_row, scale, put, get):
        buffers = (grama, gramb)
        width = norm_row.shape[1]
        total = jnp.zeros((4 * probes, width), jnp.float32)
        buffers[0][:, 0:width] = mxu(twin[0], other(), NT)
        for i in range(tiles):
            if i + 1 < tiles:
                buffers[(i + 1) % 2][:, 0:width] = mxu(twin[i + 1], other(), NT)
            for low in range(0, TILE, PIECE):
                rows = slice(low, low + PIECE)
                value = affinity(buffers[i % 2][rows, 0:width], ncol[i, rows], norm_row)
                if scale is not None:
                    value = value * scale
                put(i, rows, value.astype(jnp.bfloat16))
            acc[:, cs(i)] += mxu(theirs, get(i), NT)
            total = total + mxu(mown[:, cs(i)], get(i), NN)
        return total

    def chunk_span(s):
        width = fold * TILE
        return pl.ds(pl.multiple_of(s * width, width), width)

    def block_panels(block, s, other, theirs, norm_row):
        def put(i, rows, value):
            kmat[block, s, i, rows] = value

        return panels(other, theirs, norm_row, None, put, lambda i: kmat[block, s, i])

    acc[...] = jnp.zeros_like(acc)

    @pl.loop(0, chunks)
    def _(s):
        span = chunk_span(s)
        block_panels(0, s, lambda: pts[piece(s)].reshape(fold * TILE, pts.shape[2]),
                     mown[:, span], vec1[probes : probes + 1, span])

    def band(block):
        vec_in(0, block).wait_recv()

        @pl.loop(0, chunks)
        def _(s):
            pts_in(block, s).wait_recv()
            if block == 1:
                @pl.when(odd)
                def _():
                    forward_pts(s).start()

            span = chunk_span(s)
            theirs = split_rows(vin1[block, 0:probes, span], True)
            total = block_panels(1 + block, s, lambda: pin[block, piece(s)].reshape(fold * TILE, pts.shape[2]),
                                 theirs, vin1[block, probes : probes + 1, span])
            hout1[block, :, span] = merge_rows(total, probes, True)

        hand(0, block).start()

    def cross(k):
        cvec(0, k).wait_recv()
        cpts(k).wait_recv()
        wide = cap * TILE
        lane_tile = lax.broadcasted_iota(jnp.int32, (1, wide), 1) // TILE
        live = jnp.zeros((1, wide), jnp.float32)
        for c in range(cap):
            live = live + jnp.where(tile_id(g, down(k), c) >= 0, 1.0, 0.0) * jnp.where(lane_tile == c, 1.0, 0.0)
        theirs = split_rows(cvi1[k - 1, 0:probes], True)

        def put(i, rows, value):
            kc[k - 1, i, rows] = value

        total = panels(lambda: inp[k - 1].reshape(wide, pts.shape[2]), theirs,
                       cvi1[k - 1, probes : probes + 1], live, put, lambda i: kc[k - 1, i])
        cho1[k - 1] = merge_rows(total, probes, True)
        chand(0, k).start()

    @pl.when(odd)
    def _():
        band(0)

    cross(1)

    @pl.when(jnp.logical_and(even, has_first))
    def _():
        band(0)

    @pl.when(has_second)
    def _():
        band(1)

    for k in range(2, groups):
        cross(k)

    def gather_backs(r, total):
        incoming, cross_in = (hin1, chi1) if r == 0 else (hin2, chi2)
        for k in range(1, groups):
            chand(r, k).wait_recv()
        for k in range(1, groups):
            for c in range(cap):
                named = tile_id(up(k), g, c)
                part = cross_in[k - 1, :, cs(c)]
                for q in range(tiles):
                    total[q] = total[q] + jnp.where(named == q, 1.0, 0.0) * part
        return total

    def wait_hands(r):
        for slot, cond in ((0, has_next), (1, has_far)):
            @pl.when(cond)
            def _():
                hand_in(r, slot).wait_recv()

    for slot, cond in ((0, has_next), (1, has_far)):
        @pl.when(jnp.logical_not(cond))
        def _():
            hin1[slot] = jnp.zeros((2 * probes, cols), jnp.float32)
            hin2[slot] = jnp.zeros((probes, cols), jnp.float32)

    wait_hands(0)
    sums = [merge_rows(acc[:, cs(q)], probes, True) + hin1[0, :, cs(q)] + hin1[1, :, cs(q)] for q in range(tiles)]
    sums = gather_backs(0, sums)
    for q in range(tiles):
        base = tgt[:, cs(q)]
        degree = sums[q][probes : 2 * probes]
        applied = noise_level * base + value_weight * (degree * base - sums[q][0:probes])
        vec2[:, cs(q)] = applied
        deg[:, cs(q)] = degree
    for k in range(1, groups):
        for c in range(cap):
            named = tile_id(up(k), g, c)
            total = jnp.zeros((probes, TILE), jnp.float32)
            for q in range(tiles):
                total = total + jnp.where(named == q, 1.0, 0.0) * vec2[:, cs(q)]
            cvo2[k - 1, :, cs(c)] = total
    send_vectors(1)

    for j in range(tiles):
        rows = split_rows(vec2[:, cs(j)], False)
        mown[0 : 2 * probes, cs(j)] = rows
    two = 2 * probes

    def span_of(s):
        return slice(s * fold * TILE, (s + 1) * fold * TILE)

    def whole(block, s):
        return kmat[block, s].reshape(cols, fold * TILE)

    def own_sums(rows, block):
        return sum(merge_rows(mxu(rows[0:two, span_of(s)], whole(block, s), NT), probes, False) for s in range(chunks))

    acc2[...] = own_sums(mown, 0)

    def merged(q):
        return acc2[:, cs(q)]

    quad_local = jnp.zeros((probes, 1), jnp.float32)
    for q in range(tiles):
        quad_local = quad_local + jnp.sum(vec2[:, cs(q)] * merged(q), axis=1, keepdims=True)

    def band_again(block):
        vec_in(1, block).wait_recv()
        for j in range(tiles):
            mrem[0:two, cs(j)] = split_rows(vin2[block, :, cs(j)], False)
        for s in range(chunks):
            hout2[block, :, span_of(s)] = merge_rows(mxu(mown[0:two], whole(1 + block, s), NN), probes, False)
        hand(1, block).start()
        acc2[...] += own_sums(mrem, 1 + block)

    def cross_again(k):
        cvec(1, k).wait_recv()
        for c in range(cap):
            mc[k - 1, 0:two, cs(c)] = split_rows(cvi2[k - 1, :, cs(c)], False)
        value = kc[k - 1].reshape(cols, cap * TILE)
        cho2[k - 1] = merge_rows(mxu(mown[0:two], value, NN), probes, False)
        acc2[...] += merge_rows(mxu(mc[k - 1, 0:two], value, NT), probes, False)
        chand(1, k).start()

    for block in range(2):
        @pl.when(has_block[block])
        def _():
            band_again(block)

    for k in range(1, groups):
        cross_again(k)

    parts = [jnp.zeros((probes, 1), jnp.float32) for _ in range(5)]
    for q in range(tiles):
        base, applied, degree = tgt[:, cs(q)], vec2[:, cs(q)], deg[:, cs(q)]
        terms = (base * base, base * applied, applied * applied, degree * applied * applied, applied * merged(q))
        parts = [old + jnp.sum(term, axis=1, keepdims=True) for old, term in zip(parts, terms)]
    quad = 2.0 * parts[4] - quad_local
    curved = noise_level * parts[2] + value_weight * (parts[3] - quad)
    lane = lax.broadcasted_iota(jnp.int32, (probes, 128), 1)
    message = jnp.zeros((probes, 128), jnp.float32)
    for index, part in enumerate((parts[0], parts[1], parts[2], curved)):
        message = message + jnp.where(lane == index, part, 0.0)
    red1o[...] = message

    def reduce_one(k):
        return remote(red1o, red1.at[k - 1], r1send.at[k - 1], r1recv.at[k - 1], {"group": up(k)})

    def reduce_two(k):
        return remote(red2o, red2.at[k - 1], r2send.at[k - 1], r2recv.at[k - 1], {"dev": lax.rem(d + k, devs)})

    for k in range(1, groups):
        reduce_one(k).start()
    for k in range(1, groups):
        reduce_one(k).wait_recv()
    for k in range(1, groups):
        message = message + red1[k - 1]
    red2o[...] = message
    for k in range(1, devs):
        reduce_two(k).start()

    wait_hands(1)
    sums = [merged(q) + hin2[0, :, cs(q)] + hin2[1, :, cs(q)] for q in range(tiles)]
    sums = gather_backs(1, sums)
    for q in range(tiles):
        applied, degree = vec2[:, cs(q)], deg[:, cs(q)]
        res1[:, cs(q)] = noise_level * applied + value_weight * (degree * applied - sums[q])
    for k in range(1, devs):
        reduce_two(k).wait_recv()
    for k in range(1, devs):
        message = message + red2[k - 1]
    norm0, curv0, app_sq, app_curv = [
        jnp.sum(jnp.where(lane == index, message, 0.0), axis=1, keepdims=True) for index in range(4)
    ]
    step0 = norm0 / curv0
    norm1 = norm0 - 2.0 * step0 * curv0 + step0 * step0 * app_sq
    mix = 1.0 + norm1 / norm0
    curv1 = mix * mix * curv0 - 2.0 * mix * step0 * app_sq + step0 * step0 * app_curv
    step1 = norm1 / curv1
    for q in range(tiles):
        base, applied, twice = tgt[:, cs(q)], vec2[:, cs(q)], res1[:, cs(q)]
        sol0[:, cs(q)] = step0 * base
        sol1[:, cs(q)] = step1 * (mix * base - step0 * applied)
        left = (base - step0 * applied) - step1 * (mix * applied - step0 * twice)
        res1[:, cs(q)] = left - step0 * base

    for r in range(2):
        for which, cond in ((0, has_next), (1, has_far)):
            @pl.when(cond)
            def _():
                vec_copy(r, which).wait_send()
        for block in range(2):
            @pl.when(has_block[block])
            def _():
                hand(r, block).wait_send()
        for k in range(1, groups):
            cvec(r, k).wait_send()
            chand(r, k).wait_send()
    for k in range(1, groups):
        cpts(k).wait_send()
        reduce_one(k).wait_send()
    for k in range(1, devs):
        reduce_two(k).wait_send()

    @pl.when(has_far)
    def _():
        for s in range(chunks):
            far_pts(s).wait_send()

    @pl.when(even)
    def _():
        for s in range(chunks):
            mate_pts(s).wait_send()

    @pl.when(jnp.logical_and(odd, has_second))
    def _():
        for s in range(chunks):
            forward_pts(s).wait_send()


def on_device(points, targets, partner_tiles):
    groups, devs, _, cap = partner_tiles.shape
    rows, features = points.shape
    tiles = rows // TILE
    probes = targets.shape[0]
    peers = groups - 1
    f32, bf16 = jnp.float32, jnp.bfloat16
    v = pltpu.VMEM
    dma = pltpu.SemaphoreType.DMA
    wide = cap * TILE
    two = 2 * probes
    fold = 2 if tiles % 2 == 0 else 1
    span = max(fold, cap) * TILE
    scratch = [
        v((2, tiles, TILE, features), bf16),
        v((peers, cap, TILE, features), bf16),
        v((peers, cap, TILE, features), bf16),
        v((3, tiles // fold, tiles, TILE, fold * TILE), bf16),
        v((peers, tiles, TILE, wide), bf16),
        v((tiles, TILE, 1), f32),
        v((tiles, TILE, features), bf16),
        v((TILE, span), f32),
        v((TILE, span), f32),
        v((two, rows), f32),
        v((2, two, rows), f32),
        v((peers, two, wide), f32),
        v((peers, two, wide), f32),
        v((probes, rows), f32),
        v((2, probes, rows), f32),
        v((peers, probes, wide), f32),
        v((peers, probes, wide), f32),
        v((2, two, rows), f32),
        v((2, two, rows), f32),
        v((peers, two, wide), f32),
        v((peers, two, wide), f32),
        v((2, probes, rows), f32),
        v((2, probes, rows), f32),
        v((peers, probes, wide), f32),
        v((peers, probes, wide), f32),
        v((2 * two, rows), bf16),
        v((2 * two, rows), bf16),
        v((peers, 2 * two, wide), bf16),
        v((2 * two, rows), f32),
        v((probes, rows), f32),
        v((probes, rows), f32),
        v((probes, 128), f32),
        v((peers, probes, 128), f32),
        v((probes, 128), f32),
        v((devs - 1, probes, 128), f32),
        dma((2, tiles)), dma((2, tiles)), dma((peers,)), dma((peers,)),
        dma((2, 2)), dma((2, 2)), dma((2, peers)), dma((2, peers)),
        dma((2, 2)), dma((2, 2)), dma((2, peers)), dma((2, peers)),
        dma((peers,)), dma((peers,)), dma((devs - 1,)), dma((devs - 1,)),
    ]
    pairs = rows * rows * 3 + rows * wide * peers
    sol0, sol1, res1 = pl.pallas_call(
        functools.partial(kernel, groups, devs, cap, probes, tiles),
        out_shape=(jax.ShapeDtypeStruct(targets.shape, f32),) * 3,
        in_specs=[
            pl.BlockSpec(memory_space=pltpu.SMEM),
            pl.BlockSpec(memory_space=pltpu.VMEM),
            pl.BlockSpec(memory_space=pltpu.VMEM),
        ],
        out_specs=(pl.BlockSpec(memory_space=pltpu.VMEM),) * 3,
        scratch_shapes=scratch,
        compiler_params=pltpu.CompilerParams(
            collective_id=0, has_side_effects=True, vmem_limit_bytes=56 * 1024 * 1024
        ),
        cost_estimate=pl.CostEstimate(flops=2 * features * pairs, bytes_accessed=rows * features * 2, transcendentals=pairs),
        name="graph_cg",
    )(jnp.transpose(partner_tiles, (0, 2, 3, 1)), points.reshape(tiles, TILE, features), targets)
    return (sol0 + sol1, sol0 + res1)


def solution(mesh):
    return jax.shard_map(
        on_device,
        mesh=mesh,
        in_specs=(P(("group", "dev"), None), P(None, ("group", "dev")), P()),
        out_specs=(P(None, ("group", "dev")), P(None, ("group", "dev"))),
        check_vma=False,
    )
```

```python
import functools

import jax
import jax.numpy as jnp
from jax import lax
from jax.experimental import pallas as pl
from jax.experimental.pallas import tpu as pltpu
from jax.sharding import PartitionSpec as P

TILE = 256

length_scale = 3.9
noise_level = 1.0
coupling_weight = 0.5
value_weight = coupling_weight * 4.0 / length_scale**5
PIECE = 32
MESH = pl.DeviceIdType.MESH
NT = (((1,), (1,)), ((), ()))
NN = (((1,), (0,)), ((), ()))


def mxu(left, right, dims):
    return lax.dot_general(left, right, dims, preferred_element_type=jnp.float32)


def split_rows(values, ones):
    high = values.astype(jnp.bfloat16).astype(jnp.float32)
    pieces = [high, values - high]
    if ones:
        pieces += [jnp.ones_like(values), jnp.zeros_like(values)]
    return jnp.concatenate(pieces, axis=0).astype(jnp.bfloat16)


def merge_rows(summed, probes, ones):
    coupled = summed[0:probes] + summed[probes : 2 * probes]
    if ones:
        return jnp.concatenate([coupled, summed[2 * probes : 3 * probes]], axis=0)
    return coupled


def kernel(groups, devs, cap, probes, tiles,
           tab, pts, tgt, sol0, sol1, res1,
           pin, outp, inp, kmat, kc, ncol, twin, grama, gramb, vec1, vin1, cvo1, cvi1, vec2, vin2, cvo2, cvi2,
           hout1, hin1, cho1, chi1, hout2, hin2, cho2, chi2,
           mown, mrem, mc, acc, acc2, deg, red1o, red1, red2o, red2,
           psend, precv, cpsend, cprecv, vsend, vrecv, cvsend, cvrecv,
           hsend, hrecv, chsend, chrecv, r1send, r1recv, r2send, r2recv):
    g = lax.axis_index("group")
    d = lax.axis_index("dev")
    par = lax.rem(d, 2)
    odd = par == 1
    even = par == 0
    peers = groups - 1
    cols = tiles * TILE

    def tile_id(owner, other, c):
        return tab[owner, other, c, d]

    def up(k):
        return lax.rem(g + k, groups)

    def down(k):
        return lax.rem(g + groups - k, groups)

    def cs(j):
        return slice(j * TILE, (j + 1) * TILE)

    barrier = pltpu.get_barrier_semaphore()
    for k in range(1, groups):
        pl.semaphore_signal(barrier, inc=1, device_id={"group": up(k)}, device_id_type=MESH)
    for k in range(1, devs):
        pl.semaphore_signal(barrier, inc=1, device_id={"dev": lax.rem(d + k, devs)}, device_id_type=MESH)

    @pl.loop(0, tiles)
    def _(i):
        wide = pts[i].astype(jnp.float32)
        twin[i] = pts[i] * jnp.asarray(-2.0, pts.dtype)
        ncol[i] = jnp.sum(wide * wide, axis=1, keepdims=True)

    for j in range(tiles):
        wide = pts[j].astype(jnp.float32)
        squares = wide * wide
        high = squares.astype(jnp.bfloat16)
        low = (squares - high.astype(jnp.float32)).astype(jnp.bfloat16)
        ones = jnp.ones((16, wide.shape[1]), jnp.bfloat16)
        sums = mxu(ones, high, NT) + mxu(ones, low, NT)
        vec1[0:probes, cs(j)] = tgt[:, cs(j)]
        vec1[probes : 2 * probes, cs(j)] = sums[0:probes]
        rows = split_rows(tgt[:, cs(j)], True)
        mown[:, cs(j)] = rows
    for k in range(1, groups):
        for c in range(cap):
            named = tile_id(up(k), g, c)
            outp[k - 1, c] = pts[jnp.maximum(named, 0)]
            total = jnp.zeros((2 * probes, TILE), jnp.float32)
            for q in range(tiles):
                total = total + jnp.where(named == q, 1.0, 0.0) * vec1[:, cs(q)]
            cvo1[k - 1, :, cs(c)] = total

    pl.semaphore_wait(barrier, groups + devs - 2)

    def remote(src, dst, ssem, rsem, where):
        return pltpu.make_async_remote_copy(
            src_ref=src, dst_ref=dst, send_sem=ssem, recv_sem=rsem, device_id=where, device_id_type=MESH
        )

    has_next = d + 1 < devs
    far = jnp.where(odd, jnp.minimum(d + 2, devs - 1), jnp.maximum(d - 2, 0))
    has_far = jnp.logical_or(jnp.logical_and(odd, d + 2 < devs), jnp.logical_and(even, d >= 2))
    nxt = jnp.minimum(d + 1, devs - 1)
    has_first = jnp.logical_or(odd, d + 2 < devs)
    has_second = d >= 2
    first_owner = jnp.where(odd, jnp.maximum(d - 1, 0), jnp.minimum(d + 2, devs - 1))
    second_owner = jnp.where(odd, jnp.maximum(d - 2, 0), jnp.maximum(d - 1, 0))
    has_block = (has_first, has_second)
    block_owner = (first_owner, second_owner)
    block_slot = (1 - par, par)

    def vec_copy(r, which):
        src, dst = (vec1, vin1) if r == 0 else (vec2, vin2)
        return remote(src, dst.at[par], vsend.at[r, which], vrecv.at[r, par], {"dev": (nxt, far)[which]})

    def vec_in(r, block):
        src, dst = (vec1, vin1) if r == 0 else (vec2, vin2)
        return remote(src, dst.at[block], vsend.at[r, 0], vrecv.at[r, block], {"dev": nxt})

    def cvec(r, k):
        src, dst = (cvo1, cvi1) if r == 0 else (cvo2, cvi2)
        return remote(src.at[k - 1], dst.at[k - 1], cvsend.at[r, k - 1], cvrecv.at[r, k - 1], {"group": up(k)})

    def hand(r, block):
        src, dst = (hout1, hin1) if r == 0 else (hout2, hin2)
        slot = block_slot[block]
        return remote(src.at[block], dst.at[slot], hsend.at[r, block], hrecv.at[r, slot],
                      {"dev": block_owner[block]})

    def hand_in(r, slot):
        src, dst = (hout1, hin1) if r == 0 else (hout2, hin2)
        return remote(src.at[0], dst.at[slot], hsend.at[r, 0], hrecv.at[r, slot], {"dev": nxt})

    def chand(r, k):
        src, dst = (cho1, chi1) if r == 0 else (cho2, chi2)
        return remote(src.at[k - 1], dst.at[k - 1], chsend.at[r, k - 1], chrecv.at[r, k - 1], {"group": down(k)})

    def cpts(k):
        return remote(outp.at[k - 1], inp.at[k - 1], cpsend.at[k - 1], cprecv.at[k - 1], {"group": up(k)})

    fold = 2 if tiles % 2 == 0 else 1
    chunks = tiles // fold

    def piece(s):
        return pl.ds(s * fold, fold)

    def far_pts(s):
        return remote(pts.at[piece(s)], pin.at[par, piece(s)], psend.at[1, s], precv.at[par, s], {"dev": far})

    def mate_pts(s):
        return remote(pts.at[piece(s)], pin.at[0, piece(s)], psend.at[0, s], precv.at[0, s], {"dev": nxt})

    def forward_pts(s):
        return remote(pin.at[1, piece(s)], pin.at[1, piece(s)], psend.at[0, s], precv.at[1, s],
                      {"dev": jnp.maximum(d - 1, 0)})

    def pts_in(block, s):
        return remote(pts.at[piece(s)], pin.at[block, piece(s)], psend.at[0, s], precv.at[block, s], {"dev": nxt})

    def send_vectors(r):
        for which, cond in ((0, has_next), (1, has_far)):
            @pl.when(cond)
            def _():
                vec_copy(r, which).start()
        for k in range(1, groups):
            cvec(r, k).start()

    send_vectors(0)
    for k in range(1, groups):
        cpts(k).start()

    @pl.when(even)
    def _():
        for s in range(chunks):
            mate_pts(s).start()

    @pl.when(has_far)
    def _():
        for s in range(chunks):
            far_pts(s).start()

    def affinity(inner, norm_col, norm_row):
        dist_sq = jnp.maximum((norm_col + norm_row) + inner, 1e-30)
        near = jnp.maximum(length_scale - dist_sq * lax.rsqrt(dist_sq), 0.0)
        square = near * near
        return square * square * (1.25 * length_scale - near)

    def panels(other, theirs, norm_row, scale, put, get):
        buffers = (grama, gramb)
        width = norm_row.shape[1]
        total = jnp.zeros((4 * probes, width), jnp.float32)
        buffers[0][:, 0:width] = mxu(twin[0], other(), NT)
        for i in range(tiles):
            if i + 1 < tiles:
                buffers[(i + 1) % 2][:, 0:width] = mxu(twin[i + 1], other(), NT)
            for low in range(0, TILE, PIECE):
                rows = slice(low, low + PIECE)
                value = affinity(buffers[i % 2][rows, 0:width], ncol[i, rows], norm_row)
                if scale is not None:
                    value = value * scale
                put(i, rows, value.astype(jnp.bfloat16))
            acc[:, cs(i)] += mxu(theirs, get(i), NT)
            total = total + mxu(mown[:, cs(i)], get(i), NN)
        return total

    def chunk_span(s):
        width = fold * TILE
        return pl.ds(pl.multiple_of(s * width, width), width)

    def block_panels(block, s, other, theirs, norm_row):
        def put(i, rows, value):
            kmat[block, s, i, rows] = value

        return panels(other, theirs, norm_row, None, put, lambda i: kmat[block, s, i])

    acc[...] = jnp.zeros_like(acc)

    @pl.loop(0, chunks)
    def _(s):
        span = chunk_span(s)
        block_panels(0, s, lambda: pts[piece(s)].reshape(fold * TILE, pts.shape[2]),
                     mown[:, span], vec1[probes : probes + 1, span])

    def band(block):
        vec_in(0, block).wait_recv()

        @pl.loop(0, chunks)
        def _(s):
            pts_in(block, s).wait_recv()
            if block == 1:
                @pl.when(odd)
                def _():
                    forward_pts(s).start()

            span = chunk_span(s)
            theirs = split_rows(vin1[block, 0:probes, span], True)
            total = block_panels(1 + block, s, lambda: pin[block, piece(s)].reshape(fold * TILE, pts.shape[2]),
                                 theirs, vin1[block, probes : probes + 1, span])
            hout1[block, :, span] = merge_rows(total, probes, True)

        hand(0, block).start()

    def cross(k):
        cvec(0, k).wait_recv()
        cpts(k).wait_recv()
        wide = cap * TILE
        lane_tile = lax.broadcasted_iota(jnp.int32, (1, wide), 1) // TILE
        live = jnp.zeros((1, wide), jnp.float32)
        for c in range(cap):
            live = live + jnp.where(tile_id(g, down(k), c) >= 0, 1.0, 0.0) * jnp.where(lane_tile == c, 1.0, 0.0)
        theirs = split_rows(cvi1[k - 1, 0:probes], True)

        def put(i, rows, value):
            kc[k - 1, i, rows] = value

        total = panels(lambda: inp[k - 1].reshape(wide, pts.shape[2]), theirs,
                       cvi1[k - 1, probes : probes + 1], live, put, lambda i: kc[k - 1, i])
        cho1[k - 1] = merge_rows(total, probes, True)
        chand(0, k).start()

    @pl.when(odd)
    def _():
        band(0)

    cross(1)

    @pl.when(jnp.logical_and(even, has_first))
    def _():
        band(0)

    @pl.when(has_second)
    def _():
        band(1)

    for k in range(2, groups):
        cross(k)

    def gather_backs(r, total):
        incoming, cross_in = (hin1, chi1) if r == 0 else (hin2, chi2)
        for k in range(1, groups):
            chand(r, k).wait_recv()
        for k in range(1, groups):
            for c in range(cap):
                named = tile_id(up(k), g, c)
                part = cross_in[k - 1, :, cs(c)]
                for q in range(tiles):
                    total[q] = total[q] + jnp.where(named == q, 1.0, 0.0) * part
        return total

    def wait_hands(r):
        for slot, cond in ((0, has_next), (1, has_far)):
            @pl.when(cond)
            def _():
                hand_in(r, slot).wait_recv()

    for slot, cond in ((0, has_next), (1, has_far)):
        @pl.when(jnp.logical_not(cond))
        def _():
            hin1[slot] = jnp.zeros((2 * probes, cols), jnp.float32)
            hin2[slot] = jnp.zeros((probes, cols), jnp.float32)

    wait_hands(0)
    sums = [merge_rows(acc[:, cs(q)], probes, True) + hin1[0, :, cs(q)] + hin1[1, :, cs(q)] for q in range(tiles)]
    sums = gather_backs(0, sums)
    for q in range(tiles):
        base = tgt[:, cs(q)]
        degree = sums[q][probes : 2 * probes]
        applied = noise_level * base + value_weight * (degree * base - sums[q][0:probes])
        vec2[:, cs(q)] = applied
        deg[:, cs(q)] = degree
    for k in range(1, groups):
        for c in range(cap):
            named = tile_id(up(k), g, c)
            total = jnp.zeros((probes, TILE), jnp.float32)
            for q in range(tiles):
                total = total + jnp.where(named == q, 1.0, 0.0) * vec2[:, cs(q)]
            cvo2[k - 1, :, cs(c)] = total
    send_vectors(1)

    for j in range(tiles):
        rows = split_rows(vec2[:, cs(j)], False)
        mown[0 : 2 * probes, cs(j)] = rows
    two = 2 * probes

    def span_of(s):
        return slice(s * fold * TILE, (s + 1) * fold * TILE)

    def whole(block, s):
        return kmat[block, s].reshape(cols, fold * TILE)

    def own_sums(rows, block):
        return sum(merge_rows(mxu(rows[0:two, span_of(s)], whole(block, s), NT), probes, False) for s in range(chunks))

    acc2[...] = own_sums(mown, 0)

    def merged(q):
        return acc2[:, cs(q)]

    quad_local = jnp.zeros((probes, 1), jnp.float32)
    for q in range(tiles):
        quad_local = quad_local + jnp.sum(vec2[:, cs(q)] * merged(q), axis=1, keepdims=True)

    def band_again(block):
        vec_in(1, block).wait_recv()
        for j in range(tiles):
            mrem[0:two, cs(j)] = split_rows(vin2[block, :, cs(j)], False)
        for s in range(chunks):
            hout2[block, :, span_of(s)] = merge_rows(mxu(mown[0:two], whole(1 + block, s), NN), probes, False)
        hand(1, block).start()
        acc2[...] += own_sums(mrem, 1 + block)

    def cross_again(k):
        cvec(1, k).wait_recv()
        for c in range(cap):
            mc[k - 1, 0:two, cs(c)] = split_rows(cvi2[k - 1, :, cs(c)], False)
        value = kc[k - 1].reshape(cols, cap * TILE)
        cho2[k - 1] = merge_rows(mxu(mown[0:two], value, NN), probes, False)
        acc2[...] += merge_rows(mxu(mc[k - 1, 0:two], value, NT), probes, False)
        chand(1, k).start()

    for block in range(2):
        @pl.when(has_block[block])
        def _():
            band_again(block)

    for k in range(1, groups):
        cross_again(k)

    parts = [jnp.zeros((probes, 1), jnp.float32) for _ in range(5)]
    for q in range(tiles):
        base, applied, degree = tgt[:, cs(q)], vec2[:, cs(q)], deg[:, cs(q)]
        terms = (base * base, base * applied, applied * applied, degree * applied * applied, applied * merged(q))
        parts = [old + jnp.sum(term, axis=1, keepdims=True) for old, term in zip(parts, terms)]
    quad = 2.0 * parts[4] - quad_local
    curved = noise_level * parts[2] + value_weight * (parts[3] - quad)
    lane = lax.broadcasted_iota(jnp.int32, (probes, 128), 1)
    message = jnp.zeros((probes, 128), jnp.float32)
    for index, part in enumerate((parts[0], parts[1], parts[2], curved)):
        message = message + jnp.where(lane == index, part, 0.0)
    red1o[...] = message

    def reduce_one(k):
        return remote(red1o, red1.at[k - 1], r1send.at[k - 1], r1recv.at[k - 1], {"group": up(k)})

    def reduce_two(k):
        return remote(red2o, red2.at[k - 1], r2send.at[k - 1], r2recv.at[k - 1], {"dev": lax.rem(d + k, devs)})

    for k in range(1, groups):
        reduce_one(k).start()
    for k in range(1, groups):
        reduce_one(k).wait_recv()
    for k in range(1, groups):
        message = message + red1[k - 1]
    red2o[...] = message
    for k in range(1, devs):
        reduce_two(k).start()

    wait_hands(1)
    sums = [merged(q) + hin2[0, :, cs(q)] + hin2[1, :, cs(q)] for q in range(tiles)]
    sums = gather_backs(1, sums)
    for q in range(tiles):
        applied, degree = vec2[:, cs(q)], deg[:, cs(q)]
        res1[:, cs(q)] = noise_level * applied + value_weight * (degree * applied - sums[q])
    for k in range(1, devs):
        reduce_two(k).wait_recv()
    for k in range(1, devs):
        message = message + red2[k - 1]
    norm0, curv0, app_sq, app_curv = [
        jnp.sum(jnp.where(lane == index, message, 0.0), axis=1, keepdims=True) for index in range(4)
    ]
    step0 = norm0 / curv0
    norm1 = norm0 - 2.0 * step0 * curv0 + step0 * step0 * app_sq
    mix = 1.0 + norm1 / norm0
    curv1 = mix * mix * curv0 - 2.0 * mix * step0 * app_sq + step0 * step0 * app_curv
    step1 = norm1 / curv1
    for q in range(tiles):
        base, applied, twice = tgt[:, cs(q)], vec2[:, cs(q)], res1[:, cs(q)]
        sol0[:, cs(q)] = step0 * base
        sol1[:, cs(q)] = step1 * (mix * base - step0 * applied)
        left = (base - step0 * applied) - step1 * (mix * applied - step0 * twice)
        res1[:, cs(q)] = left - step0 * base

    for r in range(2):
        for which, cond in ((0, has_next), (1, has_far)):
            @pl.when(cond)
            def _():
                vec_copy(r, which).wait_send()
        for block in range(2):
            @pl.when(has_block[block])
            def _():
                hand(r, block).wait_send()
        for k in range(1, groups):
            cvec(r, k).wait_send()
            chand(r, k).wait_send()
    for k in range(1, groups):
        cpts(k).wait_send()
        reduce_one(k).wait_send()
    for k in range(1, devs):
        reduce_two(k).wait_send()

    @pl.when(has_far)
    def _():
        for s in range(chunks):
            far_pts(s).wait_send()

    @pl.when(even)
    def _():
        for s in range(chunks):
            mate_pts(s).wait_send()

    @pl.when(jnp.logical_and(odd, has_second))
    def _():
        for s in range(chunks):
            forward_pts(s).wait_send()


def on_device(points, targets, partner_tiles):
    groups, devs, _, cap = partner_tiles.shape
    rows, features = points.shape
    tiles = rows // TILE
    probes = targets.shape[0]
    peers = groups - 1
    f32, bf16 = jnp.float32, jnp.bfloat16
    v = pltpu.VMEM
    dma = pltpu.SemaphoreType.DMA
    wide = cap * TILE
    two = 2 * probes
    fold = 2 if tiles % 2 == 0 else 1
    span = max(fold, cap) * TILE
    scratch = [
        v((2, tiles, TILE, features), bf16),
        v((peers, cap, TILE, features), bf16),
        v((peers, cap, TILE, features), bf16),
        v((3, tiles // fold, tiles, TILE, fold * TILE), bf16),
        v((peers, tiles, TILE, wide), bf16),
        v((tiles, TILE, 1), f32),
        v((tiles, TILE, features), bf16),
        v((TILE, span), f32),
        v((TILE, span), f32),
        v((two, rows), f32),
        v((2, two, rows), f32),
        v((peers, two, wide), f32),
        v((peers, two, wide), f32),
        v((probes, rows), f32),
        v((2, probes, rows), f32),
        v((peers, probes, wide), f32),
        v((peers, probes, wide), f32),
        v((2, two, rows), f32),
        v((2, two, rows), f32),
        v((peers, two, wide), f32),
        v((peers, two, wide), f32),
        v((2, probes, rows), f32),
        v((2, probes, rows), f32),
        v((peers, probes, wide), f32),
        v((peers, probes, wide), f32),
        v((2 * two, rows), bf16),
        v((2 * two, rows), bf16),
        v((peers, 2 * two, wide), bf16),
        v((2 * two, rows), f32),
        v((probes, rows), f32),
        v((probes, rows), f32),
        v((probes, 128), f32),
        v((peers, probes, 128), f32),
        v((probes, 128), f32),
        v((devs - 1, probes, 128), f32),
        dma((2, tiles)), dma((2, tiles)), dma((peers,)), dma((peers,)),
        dma((2, 2)), dma((2, 2)), dma((2, peers)), dma((2, peers)),
        dma((2, 2)), dma((2, 2)), dma((2, peers)), dma((2, peers)),
        dma((peers,)), dma((peers,)), dma((devs - 1,)), dma((devs - 1,)),
    ]
    pairs = rows * rows * 3 + rows * wide * peers
    sol0, sol1, res1 = pl.pallas_call(
        functools.partial(kernel, groups, devs, cap, probes, tiles),
        out_shape=(jax.ShapeDtypeStruct(targets.shape, f32),) * 3,
        in_specs=[
            pl.BlockSpec(memory_space=pltpu.SMEM),
            pl.BlockSpec(memory_space=pltpu.VMEM),
            pl.BlockSpec(memory_space=pltpu.VMEM),
        ],
        out_specs=(pl.BlockSpec(memory_space=pltpu.VMEM),) * 3,
        scratch_shapes=scratch,
        compiler_params=pltpu.CompilerParams(
            collective_id=0, has_side_effects=True, vmem_limit_bytes=56 * 1024 * 1024
        ),
        cost_estimate=pl.CostEstimate(flops=2 * features * pairs, bytes_accessed=rows * features * 2, transcendentals=pairs),
        name="graph_cg",
    )(jnp.transpose(partner_tiles, (0, 2, 3, 1)), points.reshape(tiles, TILE, features), targets)
    return (sol0 + sol1, sol0 + res1)


def solution(mesh):
    return jax.shard_map(
        on_device,
        mesh=mesh,
        in_specs=(P(("group", "dev"), None), P(None, ("group", "dev")), P()),
        out_specs=(P(None, ("group", "dev")), P(None, ("group", "dev"))),
        check_vma=False,
    )
```
